32 devices in a mesh: branch: 2 (over x), cluster: 16 (over z, y, core).
Axes of the slice: x: 2, y: 2, z: 4, core: 2. Of those that a mesh axis runs over, the one named last changes fastest.
Arguments:
- charges: float32 [512, 16, 256], P(('branch', 'cluster')), may hold values from -6 to 6
- coords: float32 [512, 3, 256], P(('branch', 'cluster')), may hold values from -4 to 4
- areas: float32 [512, 256], P(('branch', 'cluster')), may hold values from 0.1 to 1
- col_basis: float32 [512, 64, 256], P(('branch', 'cluster')), may hold values from -0.375 to 0.375
- row_basis: float32 [512, 64, 256], P(('branch', 'cluster')), may hold values from -0.75 to 0.75
- leaf_up: float32 [512, 64, 64], P(('branch', 'cluster')), may hold values from -0.1875 to 0.1875
- leaf_down: float32 [512, 64, 64], P(('branch', 'cluster')), may hold values from -0.75 to 0.75
- leaf_coupling: float32 [512, 4, 64, 64], P(('branch', 'cluster')), may hold values from -0.375 to 0.375
- up_transfer: float32 [2, 4, 2, 64, 64], P('branch'), may hold values from -0.5 to 0.5
- down_transfer: float32 [2, 4, 2, 64, 64], P('branch'), may hold values from -0.75 to 0.75
- sibling_coupling: float32 [2, 4, 2, 64, 64], P('branch'), may hold values from -0.75 to 0.75
- branch_coupling: float32 [2, 1, 64, 64], P('branch'), may hold values from -0.75 to 0.75
- near_list: int32 [512, 16], P(('branch', 'cluster')), may hold values from 0 to 511, as said below
- far_list: int32 [512, 4], P(('branch', 'cluster')), may hold values from 0 to 511, as said below
Outputs:
- potential: float32 [512, 16, 256], P(('branch', 'cluster'))
The draws below stay inside these ranges and needn't reach their ends.
Inputs may be any that keep to these rules, and one draw needn't show every extreme that they name: `near_list`: row n names 16 distinct leaves of the same branch, each held by the device of leaf n or by one of its two neighbours along the cluster axis; the first entry is n itself. `far_list`: row n names 4 distinct leaves from the same window of three devices as near_list, none of them in row n of near_list.
All inputs are finite; a program needn't handle non-finite values.
Results may differ from the reference program's by a relative error of at most 0.00022.
Values sent between devices are 32-bit elements; how exact they have to be, the bound alone decides.
No kernel may reach another device: no remote copies, remote signals or barrier semaphores. Data moves between devices by JAX's collectives and lax.ppermute only.
A program may use at most 64 MiB of HBM per device.

```python
import math
import jax
import jax.numpy as jnp
from jax import lax

PANELS = 256
RANK = 64
SCEN = 16
LEAVES_DEV = 16
NEAR = 16
FAR = 4
BRANCHES = 2
CLUSTERS = 16
LEVELS = 4
LEAVES = 512


def partner_lists(key):
    shared = jax.random.fold_in(key, 7)
    leaf_ids = jnp.arange(LEAVES, dtype=jnp.int32)
    device_ids = leaf_ids // LEAVES_DEV
    cluster_pos = device_ids % CLUSTERS
    window = jnp.arange(3 * LEAVES_DEV, dtype=jnp.int32)
    candidates = (device_ids * LEAVES_DEV - LEAVES_DEV)[:, None] + window[None, :]
    neighbour_pos = cluster_pos[:, None] + window[None, :] // LEAVES_DEV - 1
    valid = (neighbour_pos >= 0) & (neighbour_pos < CLUSTERS)
    scores = jax.random.randint(shared, (LEAVES, 3 * LEAVES_DEV), 0, 1 << 20, dtype=jnp.int32) * (4 * LEAVES_DEV) + window[None, :]
    scores = jnp.where(valid, scores, -1)
    own_slot = LEAVES_DEV + leaf_ids % LEAVES_DEV
    scores = jnp.where(window[None, :] == own_slot[:, None], 1 << 30, scores)
    best_scores, order = lax.top_k(scores, NEAR + FAR)
    return jnp.take_along_axis(candidates, order, axis=1).astype(jnp.int32)


def draw_near_list(key, part):
    return partner_lists(key)[:, :NEAR]


def draw_far_list(key, part):
    return partner_lists(key)[:, NEAR:]


def block_levels(own_key, dims, cuts, least, largest):
    loudness, own = 1.0, jax.random.fold_in(own_key, 6)
    for dim, blocks in cuts:
        steps = jnp.exp(jax.random.uniform(jax.random.fold_in(own, dim), (blocks,), jnp.float32, least / len(cuts), largest / len(cuts)))
        loudness = loudness * jnp.repeat(steps, dims[dim] // blocks).reshape([-1 if axis == dim else 1 for axis in range(len(dims))])
    return loudness


def bell_draw(own_key, extent, deviation, bound, pieces=(), kind=jnp.bfloat16):
    result = deviation * jax.random.normal(own_key, extent, jnp.float32)
    if pieces:
        result = result * block_levels(own_key, extent, pieces, -0.22, 0.18)
    return jnp.clip(result, -bound, bound).astype(kind)


def setup_inputs(seed: int = 0) -> dict:
    splits = jax.random.split(jax.random.key(seed), 15)
    return {
        "charges": bell_draw(splits[0], (LEAVES, SCEN, PANELS), 1.0, 6.0, ((0, 32),), jnp.float32),
        "coords": bell_draw(splits[1], (LEAVES, 3, PANELS), 1.0, 4.0, ((0, 32),), jnp.float32),
        "areas": jnp.clip(jnp.exp(math.log(1.0) - 2.3025851 * jax.random.uniform(splits[2], (LEAVES, PANELS), jnp.float32) ** block_levels(splits[2], (LEAVES, PANELS), ((0, 32),), -0.2, 0.2)), 0.1, 1.0),
        "col_basis": bell_draw(splits[3], (LEAVES, RANK, PANELS), PANELS ** -0.5, 0.375, ((0, 32),), jnp.float32),
        "row_basis": bell_draw(splits[4], (LEAVES, RANK, PANELS), RANK ** -0.5, 0.75, ((0, 32),), jnp.float32),
        "leaf_up": bell_draw(splits[5], (LEAVES, RANK, RANK), (RANK * LEAVES_DEV) ** -0.5, 0.1875, ((0, 32),), jnp.float32),
        "leaf_down": bell_draw(splits[6], (LEAVES, RANK, RANK), RANK ** -0.5, 0.75, ((0, 32),), jnp.float32),
        "leaf_coupling": bell_draw(splits[7], (LEAVES, FAR, RANK, RANK), (RANK * FAR) ** -0.5, 0.375, ((0, 32),), jnp.float32),
        "up_transfer": bell_draw(splits[8], (BRANCHES, LEVELS, 2, RANK, RANK), (2 * RANK) ** -0.5, 0.5, ((0, 2),), jnp.float32),
        "down_transfer": bell_draw(splits[9], (BRANCHES, LEVELS, 2, RANK, RANK), RANK ** -0.5, 0.75, ((0, 2),), jnp.float32),
        "sibling_coupling": bell_draw(splits[10], (BRANCHES, LEVELS, 2, RANK, RANK), RANK ** -0.5, 0.75, ((0, 2),), jnp.float32),
        "branch_coupling": bell_draw(splits[11], (BRANCHES, BRANCHES - 1, RANK, RANK), (RANK * (BRANCHES - 1)) ** -0.5, 0.75, ((0, 2),), jnp.float32),
        "near_list": draw_near_list(jax.random.fold_in(splits[14], 71), 0),
        "far_list": draw_far_list(jax.random.fold_in(splits[14], 71), 0),
    }


highest = lax.Precision.HIGHEST
reg_square = 0.01
inv_four_pi = 0.25 / math.pi

def near_group(target_coords, near_ids, charges, coords, areas):
    group_size = target_coords.shape[0]
    running = jnp.zeros((group_size, SCEN, PANELS), jnp.float32)
    for slot_index in range(NEAR):
        column_ids = near_ids[:, slot_index]
        src_charge = charges[column_ids]
        src_coords = coords[column_ids]
        src_area = areas[column_ids]
        dist_square = jnp.zeros((group_size, PANELS, PANELS), jnp.float32)
        for axis_index in range(3):
            offset = target_coords[:, axis_index, :, None] - src_coords[:, axis_index, None, :]
            dist_square = dist_square + offset * offset
        kernel = src_area[:, None, :] * inv_four_pi / jnp.sqrt(dist_square + reg_square)
        running = running + jnp.einsum('lpq,lsq->lsp', kernel, src_charge, precision=highest)
    return running

def reference(charges, coords, areas, col_basis, row_basis, leaf_up, leaf_down, leaf_coupling, up_transfer, down_transfer, sibling_coupling, branch_coupling, near_list, far_list):
    device_count = BRANCHES * CLUSTERS

    def per_group(inputs):
        return near_group(inputs[0], inputs[1], charges, coords, areas)
    near_part = lax.map(per_group, (coords.reshape(device_count, LEAVES_DEV, 3, PANELS), near_list.reshape(device_count, LEAVES_DEV, NEAR)))
    near_part = near_part.reshape(LEAVES, SCEN, PANELS)
    leaf_coef = jnp.einsum('nkp,nsp->nks', col_basis, charges, precision=highest)
    far_coef = leaf_coef[far_list]
    leaf_local = jnp.einsum('njac,njcs->nas', leaf_coupling, far_coef, precision=highest)
    node_coef = jnp.einsum('nac,ncs->nas', leaf_up, leaf_coef, precision=highest)
    node_coef = node_coef.reshape(BRANCHES, CLUSTERS, LEAVES_DEV, RANK, SCEN).sum(axis=2)
    upward = [node_coef]
    current = node_coef
    for level_index in range(LEVELS):
        paired = current.reshape(BRANCHES, -1, 2, RANK, SCEN)
        current = jnp.einsum('bac,bgcs->bgas', up_transfer[:, level_index, 0], paired[:, :, 0], precision=highest) + jnp.einsum('bac,bgcs->bgas', up_transfer[:, level_index, 1], paired[:, :, 1], precision=highest)
        upward.append(current)
    branch_roots = current[:, 0]
    partner_ids = (jnp.arange(BRANCHES)[:, None] + 1 + jnp.arange(BRANCHES - 1)[None, :]) % BRANCHES
    downward = jnp.einsum('biac,bics->bas', branch_coupling, branch_roots[partner_ids], precision=highest)[:, None]
    for level_index in reversed(range(LEVELS)):
        level_coef = upward[level_index]
        node_count = level_coef.shape[1]
        sibling_coef = level_coef.reshape(BRANCHES, node_count // 2, 2, RANK, SCEN)[:, :, ::-1].reshape(BRANCHES, node_count, RANK, SCEN)
        parity = jnp.arange(node_count) % 2
        sib_mats = sibling_coupling[:, level_index][:, parity]
        down_mats = down_transfer[:, level_index][:, parity]
        parent = jnp.repeat(downward, 2, axis=1)
        downward = jnp.einsum('bgac,bgcs->bgas', sib_mats, sibling_coef, precision=highest) + jnp.einsum('bgac,bgcs->bgas', down_mats, parent, precision=highest)
    leaf_parent = jnp.repeat(downward.reshape(BRANCHES * CLUSTERS, RANK, SCEN), LEAVES_DEV, axis=0)
    leaf_total = leaf_local + jnp.einsum('nac,ncs->nas', leaf_down, leaf_parent, precision=highest)
    return jnp.einsum('nkp,nks->nsp', row_basis, leaf_total, precision=highest) + near_part
```

```python
import functools
import math

import jax
import jax.numpy as jnp
from jax import lax
from jax.experimental import pallas as pl
from jax.experimental.pallas import tpu as pltpu
from jax.sharding import PartitionSpec as P

f32, bf16 = jnp.float32, jnp.bfloat16
reg_square = 0.01
inv_four_pi = 0.25 / math.pi
dims = 3
ahead = 4
chunk = 2 * ahead
vmem = pl.BlockSpec(memory_space=pltpu.VMEM)
smem = pl.BlockSpec(memory_space=pltpu.SMEM)
params = pltpu.CompilerParams(vmem_limit_bytes=20 * 2**20)
depth = 32


def split(x):
    high = x.astype(bf16)
    return high, (x - high.astype(f32)).astype(bf16)


def split_three(x):
    high, rest = x.astype(bf16), None
    rest = x - high.astype(f32)
    middle = rest.astype(bf16)
    return high, middle, (rest - middle.astype(f32)).astype(bf16)


def dot_split(a, b, contract):
    rows = a.shape[0]
    a_high, a_low = split(a)
    b_high, b_low = split(b)
    numbers = (((1,), (contract,)), ((), ()))
    first = lax.dot_general(
        jnp.concatenate([a_high, a_low], axis=0), b_high, numbers, preferred_element_type=f32
    )
    second = lax.dot_general(a_high, b_low, numbers, preferred_element_type=f32)
    return first[:rows] + first[rows:] + second


def pieces_of(coords, source):
    norm = coords[0] * coords[0] + coords[1] * coords[1] + coords[2] * coords[2]
    if not source:
        norm = norm + reg_square
        coords = [-2.0 * c for c in coords]
    rows = []
    for c in coords:
        high, middle, low = split_three(c)
        rows += [high, middle, high, low, high, middle] if source else [high, high, middle, high, low, middle]
    one = jnp.ones_like(norm).astype(bf16)
    norms = list(split_three(norm))
    rows += [one, one, one] + norms if source else norms + [one, one, one]
    return [row.astype(f32) for row in rows]


def stage_coords(coords, origin, source, out_ref, base):
    leaves, panels = coords[0].shape
    rows = pieces_of([c - o for c, o in zip(coords, origin)], source)
    zeros = jnp.zeros((depth - len(rows), panels), f32)
    for leaf in range(leaves):
        group = [row[leaf : leaf + 1] for row in rows] + [zeros]
        out_ref[base + leaf] = jnp.concatenate(group, axis=0).astype(bf16)


def coef_place(leaf, scen, rank, panels, first_row):
    per_row = panels // rank
    row = first_row + leaf // per_row * scen
    lane = leaf % per_row * rank
    return slice(row, row + scen), slice(lane, lane + rank)


def prep_kernel(
    charges_ref, coords_ref, areas_ref, col_ref, up_ref, near_ref, far_ref,
    pack_ref, node_ref, pairs_ref, target_ref, source_ref, charge_ref,
):
    leaves, scen, panels = charges_ref.shape
    rank = col_ref.shape[1]
    coord_row = leaves * scen
    coef_row = coord_row + leaves * dims

    node = jnp.zeros((scen, rank), f32)
    for leaf in range(leaves):
        charge = charges_ref[leaf]
        weighted = charge * (areas_ref[leaf : leaf + 1] * inv_four_pi)
        pack_ref[leaf * scen : (leaf + 1) * scen] = weighted
        high, low = split(weighted)
        charge_ref[leaf, :scen] = high
        charge_ref[leaf, scen:] = low
        coef = dot_split(charge, col_ref[leaf], 1)
        pack_ref[coef_place(leaf, scen, rank, panels, coef_row)] = coef
        node = node + dot_split(coef, up_ref[leaf], 1)
    node_ref[...] = node
    coords = [coords_ref[axis] for axis in range(dims)]
    origin = [jnp.mean(c) for c in coords]
    for axis in range(dims):
        pack_ref[coord_row + axis * leaves : coord_row + (axis + 1) * leaves] = coords[axis]
    stage_coords(coords, origin, False, target_ref, 0)
    stage_coords(coords, origin, True, source_ref, 0)

    slots = near_ref.shape[1]
    count = leaves * slots
    near = near_ref[...]
    base = near[0:1, 0:1] - leaves

    def flat(table):
        n = table.shape[1]
        spread = jnp.where(
            lax.rem(lax.broadcasted_iota(jnp.int32, (n, count), 1), n)
            == lax.broadcasted_iota(jnp.int32, (n, count), 0), 1.0, 0.0
        )
        wide = jnp.dot(table.astype(f32).astype(bf16), spread.astype(bf16), preferred_element_type=f32)
        mine = lax.broadcasted_iota(jnp.int32, (leaves, count), 1) // n == lax.broadcasted_iota(
            jnp.int32, (leaves, count), 0
        )
        return jnp.sum(jnp.where(mine, wide, 0.0), axis=0, keepdims=True)

    source = flat(near - base)
    partners = far_ref.shape[0]
    far_slots = far_ref[...].astype(jnp.int32) - jnp.broadcast_to(base, far_ref.shape)
    own_rows = jnp.broadcast_to(
        jnp.where((source >= leaves) & (source < 2 * leaves), 1.0, 0.0), (8, count)
    )
    rows = lax.broadcasted_iota(jnp.int32, (count, count), 0)
    cols = lax.broadcasted_iota(jnp.int32, (count, count), 1)
    earlier = jnp.where(rows < cols, 1.0, 0.0).astype(bf16)
    own_before = jnp.dot(own_rows.astype(bf16), earlier, preferred_element_type=f32)
    total = jnp.sum(own_rows, axis=1, keepdims=True)
    index = lax.broadcasted_iota(jnp.int32, (8, count), 1)
    spot = jnp.where(own_rows > 0.0, own_before, total + index.astype(f32) - own_before)
    chosen = jnp.where(rows == spot[:1].astype(jnp.int32), 1.0, 0.0).astype(bf16)
    kind = lax.broadcasted_iota(jnp.int32, (8, count), 0)
    values = jnp.where(kind == 0, (index // slots).astype(f32), jnp.broadcast_to(source, (8, count)))
    values = lax.dot_general(
        values.astype(bf16), chosen, (((1,), (1,)), ((), ())), preferred_element_type=f32
    )
    pairs_ref[...] = jnp.where(kind == 2, total, values).astype(jnp.int32)
    pairs_ref[4 : 4 + partners, :leaves] = far_slots


def stage_kernel(
    pairs_ref, own_ref, below_ref, above_ref, own_source_ref, own_charge_ref, coupling_ref,
    source_ref, charge_ref, local_ref, coef_ref,
):
    leaves, scen = local_ref.shape[:2]
    rank = local_ref.shape[2]
    panels = own_ref.shape[1]
    coord_row = leaves * scen
    coef_row = coord_row + leaves * dims

    def coords_of(pack_ref):
        return [
            pack_ref[coord_row + axis * leaves : coord_row + (axis + 1) * leaves]
            for axis in range(dims)
        ]

    origin = [jnp.mean(c) for c in coords_of(own_ref)]
    source_ref[leaves : 2 * leaves] = own_source_ref[...]
    charge_ref[leaves : 2 * leaves] = own_charge_ref[...]
    for place, pack_ref in enumerate((below_ref, own_ref, above_ref)):
        if place != 1:
            stage_coords(coords_of(pack_ref), origin, True, source_ref, place * leaves)
        for leaf in range(leaves):
            slot = place * leaves + leaf
            if place != 1:
                high, low = split(pack_ref[leaf * scen : (leaf + 1) * scen])
                charge_ref[slot, :scen] = high
                charge_ref[slot, scen:] = low
            coef_ref[slot] = pack_ref[coef_place(leaf, scen, rank, panels, coef_row)]
    for leaf in range(leaves):
        total = jnp.zeros((scen, rank), f32)
        for partner in range(coupling_ref.shape[1]):
            total = total + dot_split(coef_ref[pairs_ref[4 + partner, leaf]], coupling_ref[leaf, partner], 1)
        local_ref[leaf] = total


def near_kernel(halo, part, parts, pairs_ref, target_ref, source_ref, charge_ref, *refs):
    out_ref, high_ref, low_ref = refs[-3:]
    start_ref = refs[0] if len(refs) > 3 else None
    leaves, scen, panels = out_ref.shape
    shift_down = 0 if halo else leaves
    if start_ref is None:
        out_ref[...] = jnp.zeros_like(out_ref)
    else:
        out_ref[...] = start_ref[...]
    count = pairs_ref.shape[1]
    own_chunks = pairs_ref[2, 0] // chunk
    first, size = (own_chunks, count // chunk - own_chunks) if halo else (0, own_chunks)
    begin = first + size * part // parts
    end = first + size * (part + 1) // parts

    def generate(pair, slot):
        pair = jnp.minimum(pair, end * chunk - 1)
        square = lax.dot_general(
            source_ref[jnp.maximum(pairs_ref[1, pair] - shift_down, 0)],
            target_ref[pairs_ref[0, pair]],
            (((0,), (0,)), ((), ())),
            preferred_element_type=f32,
        )
        high, low = split(lax.rsqrt(square))
        high_ref[slot] = high
        low_ref[slot] = low

    def apply(pair, slot):
        target = pairs_ref[0, pair]
        charge = charge_ref[pairs_ref[1, pair] - shift_down]
        first = jnp.dot(charge, high_ref[slot], preferred_element_type=f32)
        second = jnp.dot(charge[:scen], low_ref[slot], preferred_element_type=f32)
        out_ref[target] += first[:scen] + first[scen:] + second

    @pl.when(begin < end)
    def _():
        for step in range(ahead):
            generate(begin * chunk + step, step)

        def body(step, carry):
            for half in range(2):
                base = step * chunk + half * ahead
                for lane in range(ahead):
                    generate(base + ahead + lane, (1 - half) * ahead + lane)
                    apply(base + lane, half * ahead + lane)
            return carry

        lax.fori_loop(begin, end, body, 0)


def far_kernel(
    place_ref, local_ref, siblings_ref, roots_ref, down_ref, row_ref, down_transfer_ref, sibling_ref,
    branch_ref, near_ref, out_ref,
):
    leaves, scen, panels = near_ref.shape
    rank = down_ref.shape[1]
    levels = down_transfer_ref.shape[1]
    cluster_idx = place_ref[0]
    downward = jnp.zeros((scen, rank), f32)
    for other in range(roots_ref.shape[0]):
        downward = downward + dot_split(roots_ref[other], branch_ref[0, other], 1)
    for level in reversed(range(levels)):
        parity = (cluster_idx >> level) & 1
        downward = dot_split(siblings_ref[level], sibling_ref[0, level, parity], 1) + dot_split(
            downward, down_transfer_ref[0, level, parity], 1
        )
    for leaf in range(leaves):
        total = local_ref[leaf] + dot_split(downward, down_ref[leaf], 1)
        out_ref[leaf] = near_ref[leaf] + dot_split(total, row_ref[leaf], 0)


def shift(block, axis, step):
    count = lax.axis_size(axis)
    return lax.ppermute(
        block, axis, [(i, i + step) for i in range(count) if 0 <= i + step < count]
    )


def on_device(
    charges, coords, areas, col_basis, row_basis, leaf_up, leaf_down, leaf_coupling,
    up_transfer, down_transfer, sibling_coupling, branch_coupling, near_list, far_list,
):
    leaves, scen, panels = charges.shape
    rank = col_basis.shape[1]
    clusters, branches = lax.axis_size("cluster"), lax.axis_size("branch")
    levels = up_transfer.shape[1]
    cluster_idx = lax.axis_index("cluster")
    count = near_list.size
    pack_rows = leaves * scen + leaves * dims + leaves * scen * rank // panels

    def stages(places):
        return (
            jax.ShapeDtypeStruct((places * leaves, depth, panels), bf16),
            jax.ShapeDtypeStruct((places * leaves, 2 * scen, panels), bf16),
        )

    pack, node, pairs, target, own_source, own_charge = pl.pallas_call(
        prep_kernel,
        out_shape=(
            jax.ShapeDtypeStruct((pack_rows, panels), f32),
            jax.ShapeDtypeStruct((scen, rank), f32),
            jax.ShapeDtypeStruct((8, count), jnp.int32),
            jax.ShapeDtypeStruct((leaves, depth, panels), bf16),
            *stages(1),
        ),
        in_specs=[vmem] * 7,
        out_specs=(vmem,) * 6,
        compiler_params=params,
        name="prep",
    )(charges, coords.transpose(1, 0, 2), areas, col_basis, leaf_up, near_list, far_list.T)

    below = shift(pack, "cluster", 1)
    above = shift(pack, "cluster", -1)
    out = jax.ShapeDtypeStruct((leaves, scen, panels), f32)
    entries = count * panels * panels

    def near(halo, part, parts, source, charge, start):
        args = [pairs, target, source, charge] + ([] if start is None else [start])
        return pl.pallas_call(
            functools.partial(near_kernel, halo, part, parts),
            out_shape=out,
            in_specs=[smem] + [vmem] * (len(args) - 1),
            out_specs=vmem,
            scratch_shapes=[pltpu.VMEM((chunk, panels, panels), bf16)] * 2,
            compiler_params=params,
            cost_estimate=pl.CostEstimate(
                flops=entries * 20, bytes_accessed=2**20, transcendentals=entries // 4
            ),
            name="near_halo" if halo else "near_own",
        )(*args)

    def exchange(values, level):
        return lax.ppermute(values, "cluster", [(i, i ^ 1 << level) for i in range(clusters)])

    def combine(values, sibling, level):
        parity = cluster_idx >> level & 1
        left = jnp.where(parity == 0, values, sibling)
        right = jnp.where(parity == 0, sibling, values)
        both = [
            lax.dot_general(side, up_transfer[0, level, i], (((1,), (1,)), ((), ())), precision=lax.Precision.HIGHEST)
            for i, side in enumerate((left, right))
        ]
        return both[0] + both[1]

    tie = lax.optimization_barrier
    current, siblings, done = node, [], 0

    def climb(current, work):
        level = len(siblings)
        if level < levels:
            sibling = exchange(current, level)
            work, sibling = tie((work(), sibling))
            siblings.append(sibling)
            return combine(current, sibling, level), work
        return current, work()

    current, near_part = climb(current, lambda: near(False, 0, 2, own_source, own_charge, None))
    current, near_part = climb(current, lambda: near(False, 1, 2, own_source, own_charge, near_part))

    def stage():
        return pl.pallas_call(
            stage_kernel,
            out_shape=(*stages(3), jax.ShapeDtypeStruct((leaves, scen, rank), f32)),
            in_specs=[smem] + [vmem] * 6,
            out_specs=(vmem,) * 3,
            scratch_shapes=[pltpu.VMEM((3 * leaves, scen, rank), f32)],
            compiler_params=params,
            name="stage",
        )(pairs, pack, below, above, own_source, own_charge, leaf_coupling)

    current, (source, charge, local) = climb(current, stage)
    current, near_part = climb(current, lambda: near(True, 0, 2, source, charge, near_part))
    while len(siblings) < levels:
        current, _ = climb(current, lambda: jnp.zeros(()))
    roots = [
        lax.ppermute(current, "branch", [((i + 1 + other) % branches, i) for i in range(branches)])
        for other in range(branches - 1)
    ]
    near_part, roots = tie((near(True, 1, 2, source, charge, near_part), roots))
    return pl.pallas_call(
        far_kernel,
        out_shape=out,
        in_specs=[smem] + [vmem] * 9,
        out_specs=vmem,
        compiler_params=params,
        name="far",
    )(
        cluster_idx.reshape(1).astype(jnp.int32), local, jnp.stack(siblings), jnp.stack(roots),
        leaf_down, row_basis, down_transfer, sibling_coupling, branch_coupling, near_part,
    )


def solution(mesh):
    leaf3 = P(("branch", "cluster"), None, None)
    leaf2 = P(("branch", "cluster"), None)
    leaf4 = P(("branch", "cluster"), None, None, None)
    tree = P("branch", None, None, None, None)
    in_specs = (
        leaf3, leaf3, leaf2, leaf3, leaf3, leaf3, leaf3, leaf4,
        tree, tree, tree, P("branch", None, None, None), leaf2, leaf2,
    )
    return jax.shard_map(
        on_device, mesh=mesh, in_specs=in_specs, out_specs=leaf3, check_vma=False
    )
```

```python
import functools
import math

import jax
import jax.numpy as jnp
from jax import lax
from jax.experimental import pallas as pl
from jax.experimental.pallas import tpu as pltpu
from jax.sharding import PartitionSpec as P

f32, bf16 = jnp.float32, jnp.bfloat16
reg_square = 0.01
inv_four_pi = 0.25 / math.pi
dims = 3
ahead = 8
chunk = 2 * ahead
vmem = pl.BlockSpec(memory_space=pltpu.VMEM)
smem = pl.BlockSpec(memory_space=pltpu.SMEM)
params = pltpu.CompilerParams(vmem_limit_bytes=16 * 2**20)
large = pltpu.CompilerParams(vmem_limit_bytes=58 * 2**20)
depth = 32
fine, wide = jnp.float8_e4m3fn, jnp.float8_e5m2
entry_scale, fine_scale = 2.0**13, 2.0**15
own_steps = 5


def split(x):
    high = x.astype(bf16)
    return high, (x - high.astype(f32)).astype(bf16)


def split_three(x):
    high, rest = x.astype(bf16), None
    rest = x - high.astype(f32)
    middle = rest.astype(bf16)
    return high, middle, (rest - middle.astype(f32)).astype(bf16)


def dot_split(a, b, contract):
    rows = a.shape[0]
    a_high, a_low = split(a)
    b_high, b_low = split(b)
    numbers = (((1,), (contract,)), ((), ()))
    first = lax.dot_general(
        jnp.concatenate([a_high, a_low], axis=0), b_high, numbers, preferred_element_type=f32
    )
    second = lax.dot_general(a_high, b_low, numbers, preferred_element_type=f32)
    return first[:rows] + first[rows:] + second


def pieces_of(coords, source):
    coords = [c * (1.0 / entry_scale) for c in coords]
    norm = coords[0] * coords[0] + coords[1] * coords[1] + coords[2] * coords[2]
    if not source:
        norm = norm + reg_square / entry_scale**2
        coords = [-2.0 * c for c in coords]
    rows = []
    for c in coords:
        high, middle, low = split_three(c)
        rows += [high, middle, high, low, high, middle] if source else [high, high, middle, high, low, middle]
    one = jnp.ones_like(norm).astype(bf16)
    norms = list(split_three(norm))
    rows += [one, one, one] + norms if source else norms + [one, one, one]
    return [row.astype(f32) for row in rows]


def stage_coords(coords, origin, source, out_ref, base):
    leaves, panels = coords[0].shape
    rows = pieces_of([c - o for c, o in zip(coords, origin)], source)
    zeros = jnp.zeros((depth - len(rows), panels), f32)
    for leaf in range(leaves):
        group = [row[leaf : leaf + 1] for row in rows] + [zeros]
        group = jnp.concatenate(group, axis=0)
        out_ref[base + leaf] = (group.T if source else group).astype(bf16)


def stage_charge(weighted, charge_ref, tail_ref, slot):
    scen = weighted.shape[0]
    high, low = split(weighted * (1.0 / entry_scale))
    charge_ref[slot, :scen] = high
    charge_ref[slot, scen:] = low
    weighted = weighted * fine_scale
    high = weighted.astype(wide)
    low = (weighted - high.astype(f32)).astype(wide)
    tail_ref[slot] = jnp.concatenate([high.astype(f32), low.astype(f32)], axis=0).astype(wide)


def coef_place(leaf, scen, rank, panels, first_row):
    per_row = panels // rank
    row = first_row + leaf // per_row * scen
    lane = leaf % per_row * rank
    return slice(row, row + scen), slice(lane, lane + rank)


def prep_kernel(
    cluster_ref, charges_ref, coords_ref, areas_ref, col_ref, up_ref, transfer_ref, near_ref, far_ref,
    pack_ref, nodes_ref, pairs_ref, target_ref, source_ref, charge_ref, tail_ref,
):
    leaves, scen, panels = charges_ref.shape
    rank = col_ref.shape[1]
    coord_row = leaves * scen
    coef_row = coord_row + leaves * dims

    path = None
    for level in range(transfer_ref.shape[1]):
        matrix = transfer_ref[0, level, (cluster_ref[0] >> level) & 1]
        path = matrix if path is None else dot_split(matrix, path, 0)

    node = jnp.zeros((scen, rank), f32)
    for leaf in range(leaves):
        charge = charges_ref[leaf]
        weighted = charge * (areas_ref[leaf : leaf + 1] * inv_four_pi)
        pack_ref[leaf * scen : (leaf + 1) * scen] = weighted
        stage_charge(weighted, charge_ref, tail_ref, leaf)
        coef = dot_split(charge, col_ref[leaf], 1)
        pack_ref[coef_place(leaf, scen, rank, panels, coef_row)] = coef
        node = node + dot_split(coef, up_ref[leaf], 1)
    node = jnp.concatenate([node, dot_split(node, path, 1)], axis=1)
    for device in range(nodes_ref.shape[0] // scen):
        nodes_ref[device * scen : (device + 1) * scen] = node
    coords = [coords_ref[axis] for axis in range(dims)]
    origin = [jnp.mean(c) for c in coords]
    for axis in range(dims):
        pack_ref[coord_row + axis * leaves : coord_row + (axis + 1) * leaves] = coords[axis]
    stage_coords(coords, origin, False, target_ref, 0)
    stage_coords(coords, origin, True, source_ref, 0)

    slots = near_ref.shape[1]
    count = leaves * slots
    near = near_ref[...]
    base = near[0:1, 0:1] - leaves

    def flat(table):
        n = table.shape[1]
        spread = jnp.where(
            lax.rem(lax.broadcasted_iota(jnp.int32, (n, count), 1), n)
            == lax.broadcasted_iota(jnp.int32, (n, count), 0), 1.0, 0.0
        )
        wide = jnp.dot(table.astype(f32).astype(bf16), spread.astype(bf16), preferred_element_type=f32)
        mine = lax.broadcasted_iota(jnp.int32, (leaves, count), 1) // n == lax.broadcasted_iota(
            jnp.int32, (leaves, count), 0
        )
        return jnp.sum(jnp.where(mine, wide, 0.0), axis=0, keepdims=True)

    source = flat(near - base)
    partners = far_ref.shape[0]
    far_slots = far_ref[...].astype(jnp.int32) - jnp.broadcast_to(base, far_ref.shape)
    own_rows = jnp.broadcast_to(
        jnp.where((source >= leaves) & (source < 2 * leaves), 1.0, 0.0), (8, count)
    )
    rows = lax.broadcasted_iota(jnp.int32, (count, count), 0)
    cols = lax.broadcasted_iota(jnp.int32, (count, count), 1)
    earlier = jnp.where(rows < cols, 1.0, 0.0).astype(bf16)
    own_before = jnp.dot(own_rows.astype(bf16), earlier, preferred_element_type=f32)
    total = jnp.sum(own_rows, axis=1, keepdims=True)
    index = lax.broadcasted_iota(jnp.int32, (8, count), 1)
    spot = jnp.where(own_rows > 0.0, own_before, total + index.astype(f32) - own_before)
    chosen = jnp.where(rows == spot[:1].astype(jnp.int32), 1.0, 0.0).astype(bf16)
    kind = lax.broadcasted_iota(jnp.int32, (8, count), 0)
    values = jnp.where(kind == 0, (index // slots).astype(f32), jnp.broadcast_to(source, (8, count)))
    values = lax.dot_general(
        values.astype(bf16), chosen, (((1,), (1,)), ((), ())), preferred_element_type=f32
    )
    pairs_ref[...] = jnp.where(kind == 2, total, values).astype(jnp.int32)
    pairs_ref[4 : 4 + partners, :leaves] = far_slots


def near_pairs(begin, end, base_slot, pairs_ref, target_ref, source_ref, charge_ref, tail_ref, out_ref, high_ref, low_ref):
    scen = out_ref.shape[1]

    def generate(pair, slot):
        pair = jnp.minimum(pair, end * chunk - 1)
        square = jnp.dot(
            source_ref[pairs_ref[1, pair] - base_slot],
            target_ref[pairs_ref[0, pair]],
            preferred_element_type=f32,
        )
        entry = lax.rsqrt(square)
        high = entry.astype(bf16)
        high_ref[slot] = high
        low_ref[slot] = (entry - high.astype(f32)).astype(fine)

    def apply(pair, slot):
        target = pairs_ref[0, pair]
        source = pairs_ref[1, pair] - base_slot
        first = jnp.dot(charge_ref[source], high_ref[slot], preferred_element_type=f32)
        second = jnp.dot(tail_ref[source], low_ref[slot], preferred_element_type=f32)
        out_ref[target] += (
            first[:scen] + first[scen:] + (second[:scen] + second[scen:]) * (1.0 / (entry_scale * fine_scale))
        )

    @pl.when(begin < end)
    def _():
        for step in range(ahead):
            generate(begin * chunk + step, step)

        def body(step, carry):
            for half in range(2):
                base = step * chunk + half * ahead
                for lane in range(ahead):
                    generate(base + ahead + lane, (1 - half) * ahead + lane)
                    apply(base + lane, half * ahead + lane)
            return carry

        lax.fori_loop(begin, end, body, 0)


def own_chunks(pairs_ref):
    return jnp.minimum(own_steps, pairs_ref[2, 0] // chunk)


def own_kernel(pairs_ref, target_ref, source_ref, charge_ref, tail_ref, out_ref, high_ref, low_ref):
    out_ref[...] = jnp.zeros_like(out_ref)
    near_pairs(
        0, own_chunks(pairs_ref), out_ref.shape[0], pairs_ref, target_ref, source_ref, charge_ref,
        tail_ref, out_ref, high_ref, low_ref,
    )


def rest_kernel(
    cluster_ref, pairs_ref, own_ref, chip_ref, side_ref, coupling_ref, start_ref, out_ref, local_ref,
    target_ref, source_ref, charge_ref, tail_ref, coef_ref, high_ref, low_ref,
):
    leaves, scen, panels = out_ref.shape
    rank = local_ref.shape[2]
    coord_row = leaves * scen
    coef_row = coord_row + leaves * dims

    def coords_of(pack_ref):
        return [
            pack_ref[coord_row + axis * leaves : coord_row + (axis + 1) * leaves]
            for axis in range(dims)
        ]

    own_coords = coords_of(own_ref)
    origin = [jnp.mean(c) for c in own_coords]
    stage_coords(own_coords, origin, False, target_ref, 0)
    odd = cluster_ref[0] & 1
    for pack_ref, place in ((own_ref, 1), (chip_ref, 2 - 2 * odd), (side_ref, 2 * odd)):
        base = place * leaves
        stage_coords(coords_of(pack_ref), origin, True, source_ref, base)
        for leaf in range(leaves):
            stage_charge(pack_ref[leaf * scen : (leaf + 1) * scen], charge_ref, tail_ref, base + leaf)
            coef_ref[base + leaf] = pack_ref[coef_place(leaf, scen, rank, panels, coef_row)]
    for leaf in range(leaves):
        total = jnp.zeros((scen, rank), f32)
        for partner in range(coupling_ref.shape[1]):
            total = total + dot_split(coef_ref[pairs_ref[4 + partner, leaf]], coupling_ref[leaf, partner], 1)
        local_ref[leaf] = total
    out_ref[...] = start_ref[...]
    near_pairs(
        own_chunks(pairs_ref), pairs_ref.shape[1] // chunk, 0, pairs_ref, target_ref, source_ref,
        charge_ref, tail_ref, out_ref, high_ref, low_ref,
    )


def far_kernel(
    cluster_ref, branch_idx_ref, local_ref, nodes_ref, down_ref, row_ref, transfer_ref, down_transfer_ref,
    sibling_ref, branch_ref, near_ref, out_ref,
):
    leaves, scen, panels = near_ref.shape
    rank = down_ref.shape[1]
    levels = transfer_ref.shape[1]
    branches, clusters = nodes_ref.shape[:2]
    cluster_idx, branch_idx = cluster_ref[0], branch_idx_ref[0]
    downward = jnp.zeros((scen, rank), f32)
    for other in range(branches - 1):
        partner = lax.rem(branch_idx + 1 + other, branches)
        root = jnp.sum(nodes_ref[partner], axis=0)[:, rank:]
        downward = downward + dot_split(root, branch_ref[0, other], 1)
    current = nodes_ref[branch_idx][:, :, :rank]
    siblings = []
    for level in range(levels):
        width = clusters >> level
        place = cluster_idx >> level
        siblings.append((current, place ^ 1))
        pairs = current.reshape(width // 2, 2 * scen, rank)
        left = pairs[:, :scen].reshape(width // 2 * scen, rank)
        right = pairs[:, scen:].reshape(width // 2 * scen, rank)
        current = dot_split(left, transfer_ref[0, level, 0], 1) + dot_split(
            right, transfer_ref[0, level, 1], 1
        )
        current = current.reshape(width // 2, scen, rank)
    for level in reversed(range(levels)):
        nodes, place = siblings[level]
        chosen = lax.broadcasted_iota(jnp.int32, (nodes.shape[0], 1, 1), 0) == place
        sibling = jnp.sum(jnp.where(chosen, nodes, 0.0), axis=0)
        parity = (cluster_idx >> level) & 1
        downward = dot_split(sibling, sibling_ref[0, level, parity], 1) + dot_split(
            downward, down_transfer_ref[0, level, parity], 1
        )
    for leaf in range(leaves):
        total = local_ref[leaf] + dot_split(downward, down_ref[leaf], 1)
        out_ref[leaf] = near_ref[leaf] + dot_split(total, row_ref[leaf], 0)


def on_device(
    charges, coords, areas, col_basis, row_basis, leaf_up, leaf_down, leaf_coupling,
    up_transfer, down_transfer, sibling_coupling, branch_coupling, near_list, far_list,
):
    leaves, scen, panels = charges.shape
    rank = col_basis.shape[1]
    clusters, branches = lax.axis_size("cluster"), lax.axis_size("branch")
    cluster_idx = lax.axis_index("cluster").reshape(1).astype(jnp.int32)
    branch_idx = lax.axis_index("branch").reshape(1).astype(jnp.int32)
    count = near_list.size
    pack_rows = leaves * scen + leaves * dims + leaves * scen * rank // panels

    def stages(places):
        return (
            pltpu.VMEM((places * leaves, panels, depth), bf16),
            pltpu.VMEM((places * leaves, 2 * scen, panels), bf16),
            pltpu.VMEM((places * leaves, 2 * scen, panels), wide),
        )

    slots = [pltpu.VMEM((chunk, panels, panels), kind) for kind in (bf16, fine)]
    pack, nodes, pairs, target, *own_stages = pl.pallas_call(
        prep_kernel,
        out_shape=(
            jax.ShapeDtypeStruct((pack_rows, panels), f32),
            jax.ShapeDtypeStruct((branches * clusters * scen, 2 * rank), f32),
            jax.ShapeDtypeStruct((8, count), jnp.int32),
            pltpu.VMEM((leaves, depth, panels), bf16),
            *stages(1),
        ),
        in_specs=[smem] + [vmem] * 8,
        out_specs=(vmem,) * 7,
        compiler_params=large,
        name="prep",
    )(
        cluster_idx, charges, coords.transpose(1, 0, 2), areas, col_basis, leaf_up, up_transfer,
        near_list, far_list.T,
    )

    chip = lax.ppermute(pack, "cluster", [(i, i ^ 1) for i in range(clusters)])
    across = [(i, i + 1) for i in range(1, clusters - 1, 2)]
    side = lax.ppermute(pack, "cluster", across + [(j, i) for i, j in across])
    nodes = lax.all_to_all(nodes, ("branch", "cluster"), 0, 0, tiled=True)
    nodes = nodes.reshape(branches, clusters, scen, 2 * rank)

    kept = pltpu.VMEM((leaves, scen, panels), f32)
    entries = count * panels * panels

    def cost(share):
        return pl.CostEstimate(
            flops=int(entries * 80 * share), bytes_accessed=2**20, transcendentals=int(entries * share)
        )

    near_part = pl.pallas_call(
        own_kernel,
        out_shape=kept,
        in_specs=[smem] + [vmem] * 4,
        out_specs=vmem,
        scratch_shapes=slots,
        compiler_params=params,
        cost_estimate=cost(0.3),
        name="near_own",
    )(pairs, target, *own_stages)
    near_part, local = pl.pallas_call(
        rest_kernel,
        out_shape=(kept, pltpu.VMEM((leaves, scen, rank), f32)),
        in_specs=[smem] * 2 + [vmem] * 5,
        out_specs=(vmem,) * 2,
        scratch_shapes=[
            pltpu.VMEM((leaves, depth, panels), bf16),
            *stages(3),
            pltpu.VMEM((3 * leaves, scen, rank), f32),
            *slots,
        ],
        compiler_params=params,
        cost_estimate=cost(0.7),
        name="near_rest",
    )(cluster_idx, pairs, pack, chip, side, leaf_coupling, near_part)
    return pl.pallas_call(
        far_kernel,
        out_shape=jax.ShapeDtypeStruct((leaves, scen, panels), f32),
        in_specs=[smem] * 2 + [vmem] * 9,
        out_specs=vmem,
        compiler_params=params,
        name="far",
    )(
        cluster_idx, branch_idx, local, nodes, leaf_down, row_basis, up_transfer, down_transfer,
        sibling_coupling, branch_coupling, near_part,
    )


def solution(mesh):
    leaf3 = P(("branch", "cluster"), None, None)
    leaf2 = P(("branch", "cluster"), None)
    leaf4 = P(("branch", "cluster"), None, None, None)
    tree = P("branch", None, None, None, None)
    in_specs = (
        leaf3, leaf3, leaf2, leaf3, leaf3, leaf3, leaf3, leaf4,
        tree, tree, tree, P("branch", None, None, None), leaf2, leaf2,
    )
    return jax.shard_map(
        on_device, mesh=mesh, in_specs=in_specs, out_specs=leaf3, check_vma=False
    )
```

```python
import functools
import math

import jax
import jax.numpy as jnp
from jax import lax
from jax.experimental import pallas as pl
from jax.experimental.pallas import tpu as pltpu
from jax.sharding import PartitionSpec as P

f32, bf16 = jnp.float32, jnp.bfloat16
reg_square = 0.01
inv_four_pi = 0.25 / math.pi
dims = 3
ahead = 8
chunk = 2 * ahead
vmem = pl.BlockSpec(memory_space=pltpu.VMEM)
smem = pl.BlockSpec(memory_space=pltpu.SMEM)
anywhere = pl.BlockSpec(memory_space=pl.ANY)
params = pltpu.CompilerParams(vmem_limit_bytes=24 * 2**20)
large = pltpu.CompilerParams(vmem_limit_bytes=58 * 2**20)
lines = 4
depth = 6 * 2 * lines
fine, wide = jnp.float8_e4m3fn, jnp.float8_e5m2
entry_scale, fine_scale = 2.0**13, 2.0**15
own_steps = 5


def split(x):
    high = x.astype(bf16)
    return high, (x - high.astype(f32)).astype(bf16)


def split_three(x):
    high, rest = x.astype(bf16), None
    rest = x - high.astype(f32)
    middle = rest.astype(bf16)
    return high, middle, (rest - middle.astype(f32)).astype(bf16)


def dot_split(a, b, contract):
    rows = a.shape[0]
    a_high, a_low = split(a)
    b_high, b_low = split(b)
    numbers = (((1,), (contract,)), ((), ()))
    first = lax.dot_general(
        jnp.concatenate([a_high, a_low], axis=0), b_high, numbers, preferred_element_type=f32
    )
    second = lax.dot_general(a_high, b_low, numbers, preferred_element_type=f32)
    return first[:rows] + first[rows:] + second


def coord_tiles(pack_ref, first_row, tiles):
    return [pack_ref[first_row + 2 * lines * i : first_row + 2 * lines * (i + 1)] for i in range(tiles)]


def origin_tile(tiles):
    total = sum(jnp.sum(tile, axis=1, keepdims=True) for tile in tiles)
    total = total + pltpu.roll(total, lines, 0)
    return total * (1.0 / (2 * len(tiles) * tiles[0].shape[1]))


def centred(tile, origin):
    line = lax.broadcasted_iota(jnp.int32, tile.shape, 0) & (lines - 1)
    coords = (tile - origin) * (1.0 / entry_scale)
    square = coords * coords
    norm = pltpu.roll(square, 1, 0) + pltpu.roll(square, 2, 0) + pltpu.roll(square, 3, 0)
    return coords, norm, line == dims


def stage_sources(tiles, origin, source_ref, base):
    for i, tile in enumerate(tiles):
        coords, norm, spare = centred(tile, origin)
        high, middle, low = (x.astype(f32) for x in split_three(jnp.where(spare, norm, coords)))
        high_one, middle_one = jnp.where(spare, 1.0, high), jnp.where(spare, 1.0, middle)
        rows = jnp.concatenate([high, middle, high_one, low, high_one, middle_one], axis=0)
        source_ref[base + i] = rows.T.astype(bf16)


def stage_targets(tiles, origin, target_ref):
    for i, tile in enumerate(tiles):
        coords, norm, spare = centred(tile, origin)
        tile = jnp.where(spare, norm + reg_square / entry_scale**2, -2.0 * coords)
        high, middle, low = (x.astype(f32) for x in split_three(tile))
        high_one = jnp.where(spare, 1.0, high)
        rows = [
            high_one, high_one, jnp.where(spare, high, middle), high_one, jnp.where(spare, middle, low),
            jnp.where(spare, low, middle),
        ]
        first = lax.broadcasted_iota(jnp.int32, tile.shape, 0) < lines
        for half in range(2):
            mine = [jnp.where(first if half == 0 else jnp.logical_not(first), row, 0.0) for row in rows]
            other = [pltpu.roll(row, lines, 0) for row in mine]
            for place in range(2):
                chosen = mine if place == half else other
                target_ref[(2 * i + half) * 2 + place] = jnp.concatenate(chosen, axis=0).astype(bf16)


def stage_charge(weighted, charge_ref, tail_ref, slot):
    scen = weighted.shape[0]
    high, low = split(weighted * (1.0 / entry_scale))
    charge_ref[slot, :scen] = high
    charge_ref[slot, scen:] = low
    weighted = weighted * fine_scale
    high = weighted.astype(wide)
    low = (weighted - high.astype(f32)).astype(wide)
    tail_ref[slot] = jnp.concatenate([high.astype(f32), low.astype(f32)], axis=0).astype(wide)


def coef_place(leaf, scen, rank, panels, first_row):
    per_row = panels // rank
    row = first_row + leaf // per_row * scen
    lane = leaf % per_row * rank
    return slice(row, row + scen), slice(lane, lane + rank)


def prep_kernel(
    cluster_ref, branch_ref, charges_ref, coords_ref, areas_ref, col_ref, up_ref, transfer_ref, near_ref, far_ref,
    pack_ref, terms_ref, pairs_ref, target_ref, source_ref, charge_ref, tail_ref,
):
    leaves, scen, panels = charges_ref.shape
    rank = col_ref.shape[1]
    coord_row = leaves * scen
    coef_row = coord_row + leaves * lines

    path = None
    for level in range(transfer_ref.shape[1]):
        matrix = transfer_ref[0, level, (cluster_ref[0] >> level) & 1]
        path = matrix if path is None else dot_split(matrix, path, 0)

    for leaf in range(leaves):
        charge = charges_ref[leaf]
        weighted = charge * (areas_ref[leaf : leaf + 1] * inv_four_pi)
        pack_ref[leaf * scen : (leaf + 1) * scen] = weighted
        stage_charge(weighted, charge_ref, tail_ref, leaf)
        pack_ref[coef_place(leaf, scen, rank, panels, coef_row)] = dot_split(charge, col_ref[leaf], 1)
    node = jnp.zeros((scen, rank), f32)
    per_row = panels // rank
    for group in range(leaves // per_row):
        coefs = pack_ref[coef_row + group * scen : coef_row + (group + 1) * scen]
        ups = jnp.concatenate([up_ref[group * per_row + i] for i in range(per_row)], axis=1)
        node = node + dot_split(coefs, ups, 1)
    half = scen // 2
    node, root = (
        jnp.concatenate([x[:half], x[half:]], axis=1) for x in (node, dot_split(node, path, 1))
    )
    branches = terms_ref.shape[0]
    for branch in range(branches):
        term = jnp.where(branch == branch_ref[0], node, root)
        for cluster in range(terms_ref.shape[1]):
            terms_ref[branch, cluster] = term
    nothing = jnp.zeros((1, panels), f32)
    for leaf in range(leaves):
        rows = [coords_ref[axis, leaf : leaf + 1] for axis in range(dims)] + [nothing]
        pack_ref[coord_row + lines * leaf : coord_row + lines * (leaf + 1)] = jnp.concatenate(rows, axis=0)
    tiles = coord_tiles(pack_ref, coord_row, leaves // 2)
    origin = origin_tile(tiles)
    stage_targets(tiles, origin, target_ref)
    stage_sources(tiles, origin, source_ref, 0)

    slots = near_ref.shape[1]
    count = leaves * slots
    near = near_ref[...]
    base = near[0:1, 0:1] - leaves

    def flat(table):
        n = table.shape[1]
        spread = jnp.where(
            lax.rem(lax.broadcasted_iota(jnp.int32, (n, count), 1), n)
            == lax.broadcasted_iota(jnp.int32, (n, count), 0), 1.0, 0.0
        )
        wide = jnp.dot(table.astype(f32).astype(bf16), spread.astype(bf16), preferred_element_type=f32)
        mine = lax.broadcasted_iota(jnp.int32, (leaves, count), 1) // n == lax.broadcasted_iota(
            jnp.int32, (leaves, count), 0
        )
        return jnp.sum(jnp.where(mine, wide, 0.0), axis=0, keepdims=True)

    source = flat(near - base)
    partners = far_ref.shape[0]
    far_slots = far_ref[...].astype(jnp.int32) - jnp.broadcast_to(base, far_ref.shape)
    own_rows = jnp.broadcast_to(
        jnp.where((source >= leaves) & (source < 2 * leaves), 1.0, 0.0), (8, count)
    )
    rows = lax.broadcasted_iota(jnp.int32, (count, count), 0)
    cols = lax.broadcasted_iota(jnp.int32, (count, count), 1)
    earlier = jnp.where(rows < cols, 1.0, 0.0).astype(bf16)
    own_before = jnp.dot(own_rows.astype(bf16), earlier, preferred_element_type=f32)
    total = jnp.sum(own_rows, axis=1, keepdims=True)
    index = lax.broadcasted_iota(jnp.int32, (8, count), 1)
    spot = jnp.where(own_rows > 0.0, own_before, total + index.astype(f32) - own_before)
    chosen = jnp.where(rows == spot[:1].astype(jnp.int32), 1.0, 0.0).astype(bf16)
    kind = lax.broadcasted_iota(jnp.int32, (8, count), 0)
    values = jnp.where(kind == 0, (index // slots).astype(f32), jnp.broadcast_to(source, (8, count)))
    values = lax.dot_general(
        values.astype(bf16), chosen, (((1,), (1,)), ((), ())), preferred_element_type=f32
    )
    pairs_ref[...] = jnp.where(kind == 2, total, values).astype(jnp.int32)
    pairs_ref[4 : 4 + partners, :leaves] = far_slots


def near_pairs(begin, end, base_slot, pairs_ref, target_ref, source_ref, charge_ref, tail_ref, out_ref, high_ref, low_ref):
    scen = out_ref.shape[1]

    def generate(pair, slot):
        pair = jnp.minimum(pair, end * chunk - 1)
        source = pairs_ref[1, pair] - base_slot
        square = jnp.dot(
            source_ref[source >> 1],
            target_ref[2 * pairs_ref[0, pair] + (source & 1)],
            preferred_element_type=f32,
        )
        entry = lax.rsqrt(square)
        high = entry.astype(bf16)
        high_ref[slot] = high
        low_ref[slot] = (entry - high.astype(f32)).astype(fine)

    def apply(pair, slot):
        target = pairs_ref[0, pair]
        source = pairs_ref[1, pair] - base_slot
        first = jnp.dot(charge_ref[source], high_ref[slot], preferred_element_type=f32)
        second = jnp.dot(tail_ref[source], low_ref[slot], preferred_element_type=f32)
        out_ref[target] += (
            first[:scen] + first[scen:] + (second[:scen] + second[scen:]) * (1.0 / (entry_scale * fine_scale))
        )

    @pl.when(begin < end)
    def _():
        for step in range(ahead):
            generate(begin * chunk + step, step)

        def body(step, carry):
            for half in range(2):
                base = step * chunk + half * ahead
                for lane in range(ahead):
                    generate(base + ahead + lane, (1 - half) * ahead + lane)
                    apply(base + lane, half * ahead + lane)
            return carry

        lax.fori_loop(begin, end, body, 0)


def own_chunks(pairs_ref):
    return jnp.minimum(own_steps, pairs_ref[2, 0] // chunk)


def own_kernel(pairs_ref, target_ref, source_ref, charge_ref, tail_ref, out_ref, high_ref, low_ref):
    out_ref[...] = jnp.zeros_like(out_ref)
    near_pairs(
        0, own_chunks(pairs_ref), out_ref.shape[0], pairs_ref, target_ref, source_ref, charge_ref,
        tail_ref, out_ref, high_ref, low_ref,
    )


def rest_kernel(
    cluster_ref, branch_idx_ref, pairs_ref, own_any, chip_any, side_any, coupling_any, terms_any,
    up_any, down_any, sibling_any, branch_any, leaf_down_any, row_any, start_ref, out_ref,
    own_ref, chip_ref, side_ref, coupling_ref, terms_ref, up_ref, down_ref, sibling_ref, branch_ref,
    leaf_down_ref, row_ref, target_ref, source_ref, charge_ref, tail_ref, coef_ref, high_ref, low_ref, sems,
):
    leaves, scen, panels = out_ref.shape
    rank = leaf_down_ref.shape[1]
    branches, clusters = terms_ref.shape[:2]
    levels = up_ref.shape[1]
    coord_row = leaves * scen
    coef_row = coord_row + leaves * lines
    cluster_idx, branch_idx = cluster_ref[0], branch_idx_ref[0]
    refs = (
        own_any, chip_any, side_any, terms_any, up_any, down_any, sibling_any, branch_any, coupling_any,
        leaf_down_any, row_any,
    )
    held = (
        own_ref, chip_ref, side_ref, terms_ref, up_ref, down_ref, sibling_ref, branch_ref, coupling_ref,
        leaf_down_ref, row_ref,
    )
    copies = [pltpu.make_async_copy(ref, to, sems.at[i]) for i, (ref, to) in enumerate(zip(refs, held))]
    for copy in copies:
        copy.start()

    copies[0].wait()
    tiles = coord_tiles(own_ref, coord_row, leaves // 2)
    origin = origin_tile(tiles)
    stage_targets(tiles, origin, target_ref)
    odd = cluster_idx & 1
    for i, (pack_ref, place) in enumerate(((own_ref, 1), (chip_ref, 2 - 2 * odd), (side_ref, 2 * odd))):
        if i:
            copies[i].wait()
        stage_sources(coord_tiles(pack_ref, coord_row, leaves // 2), origin, source_ref, place * (leaves // 2))
        base = place * leaves
        for leaf in range(leaves):
            stage_charge(pack_ref[leaf * scen : (leaf + 1) * scen], charge_ref, tail_ref, base + leaf)
            coef_ref[base + leaf] = pack_ref[coef_place(leaf, scen, rank, panels, coef_row)]
    for copy in copies[3:]:
        copy.wait()

    def unfold(x):
        return jnp.concatenate([x[..., :rank], x[..., rank:]], axis=-2)

    current = unfold(terms_ref[branch_idx])
    sums, chains, chain = [], [], None
    for level in range(levels):
        width = clusters >> level
        chosen = lax.broadcasted_iota(jnp.int32, (width, 1, 1), 0) == (cluster_idx >> level) ^ 1
        sums.append(jnp.sum(jnp.where(chosen, current, 0.0), axis=0))
        if level + 1 < levels:
            couples = current.reshape(width // 2, 2 * scen, rank)
            sides = [
                couples[:, side * scen : (side + 1) * scen].reshape(width // 2 * scen, rank)
                for side in range(2)
            ]
            current = dot_split(sides[0], up_ref[0, level, 0], 1) + dot_split(
                sides[1], up_ref[0, level, 1], 1
            )
            current = current.reshape(width // 2, scen, rank)
        parity = (cluster_idx >> level) & 1
        matrix = sibling_ref[0, level, parity]
        chains.append(matrix if chain is None else dot_split(chain, matrix, 0))
        matrix = down_ref[0, level, parity]
        chain = matrix if chain is None else dot_split(chain, matrix, 0)
    for other in range(branches - 1):
        partner = lax.rem(branch_idx + 1 + other, branches)
        sums.append(unfold(jnp.sum(terms_ref[partner], axis=0)))
        chains.append(dot_split(chain, branch_ref[0, other], 0))
    downward = jnp.zeros((scen, rank), f32)
    for term, matrix in zip(sums, chains):
        downward = downward + dot_split(term, matrix, 1)

    for leaf in range(leaves):
        partners = range(coupling_ref.shape[1])
        coefs = jnp.concatenate([coef_ref[pairs_ref[4 + partner, leaf]] for partner in partners], axis=1)
        matrices = jnp.concatenate([coupling_ref[leaf, partner] for partner in partners], axis=1)
        total = dot_split(coefs, matrices, 1) + dot_split(downward, leaf_down_ref[leaf], 1)
        out_ref[leaf] = start_ref[leaf] + dot_split(total, row_ref[leaf], 0)
    near_pairs(
        own_chunks(pairs_ref), pairs_ref.shape[1] // chunk, 0, pairs_ref, target_ref, source_ref,
        charge_ref, tail_ref, out_ref, high_ref, low_ref,
    )


def on_device(
    charges, coords, areas, col_basis, row_basis, leaf_up, leaf_down, leaf_coupling,
    up_transfer, down_transfer, sibling_coupling, branch_coupling, near_list, far_list,
):
    leaves, scen, panels = charges.shape
    rank = col_basis.shape[1]
    clusters, branches = lax.axis_size("cluster"), lax.axis_size("branch")
    cluster_idx = lax.axis_index("cluster").reshape(1).astype(jnp.int32)
    branch_idx = lax.axis_index("branch").reshape(1).astype(jnp.int32)
    count = near_list.size
    pack_rows = leaves * scen + leaves * lines + leaves * scen * rank // panels

    def stages(places):
        return (
            pltpu.VMEM((places * leaves // 2, panels, depth), bf16),
            pltpu.VMEM((places * leaves, 2 * scen, panels), bf16),
            pltpu.VMEM((places * leaves, 2 * scen, panels), wide),
        )

    slots = [pltpu.VMEM((chunk, panels, panels), kind) for kind in (bf16, fine)]
    terms_shape = (branches, clusters, scen // 2, 2 * rank)
    pack, terms, pairs, target, *own_stages = pl.pallas_call(
        prep_kernel,
        out_shape=(
            jax.ShapeDtypeStruct((pack_rows, panels), f32),
            jax.ShapeDtypeStruct(terms_shape, f32),
            jax.ShapeDtypeStruct((8, count), jnp.int32),
            pltpu.VMEM((2 * leaves, depth, panels), bf16),
            *stages(1),
        ),
        in_specs=[smem] * 2 + [vmem] * 8,
        out_specs=(vmem,) * 7,
        compiler_params=large,
        name="prep",
    )(
        cluster_idx, branch_idx, charges, coords.transpose(1, 0, 2), areas, col_basis, leaf_up, up_transfer,
        near_list, far_list.T,
    )

    chip = lax.ppermute(pack, "cluster", [(i, i ^ 1) for i in range(clusters)])
    across = [(i, i + 1) for i in range(1, clusters - 1, 2)]
    side = lax.ppermute(pack, "cluster", across + [(j, i) for i, j in across])
    terms = terms.reshape(branches * clusters, scen // 2, 2 * rank)
    terms = lax.all_to_all(terms, ("branch", "cluster"), 0, 0, tiled=True)
    terms = terms.reshape(terms_shape)

    kept = pltpu.VMEM((leaves, scen, panels), f32)
    entries = count * panels * panels

    def cost(share):
        return pl.CostEstimate(
            flops=int(entries * 80 * share), bytes_accessed=2**20, transcendentals=int(entries * share)
        )

    stay = functools.partial(pltpu.with_memory_space_constraint, memory_space=pltpu.HBM)
    pairs = stay(pairs)
    near_part = pl.pallas_call(
        own_kernel,
        out_shape=kept,
        in_specs=[smem] + [vmem] * 4,
        out_specs=vmem,
        scratch_shapes=slots,
        compiler_params=params,
        cost_estimate=cost(10),
        name="near_own",
    )(pairs, target, *own_stages)
    operands = (
        stay(pack), chip, side, stay(leaf_coupling), terms, stay(up_transfer), stay(down_transfer),
        stay(sibling_coupling), stay(branch_coupling), stay(leaf_down), stay(row_basis),
    )
    return pl.pallas_call(
        rest_kernel,
        out_shape=jax.ShapeDtypeStruct((leaves, scen, panels), f32),
        in_specs=[smem] * 3 + [anywhere] * len(operands) + [vmem],
        out_specs=vmem,
        scratch_shapes=[
            *(pltpu.VMEM(operand.shape, f32) for operand in operands),
            pltpu.VMEM((2 * leaves, depth, panels), bf16),
            *stages(3),
            pltpu.VMEM((3 * leaves, scen, rank), f32),
            *slots,
            pltpu.SemaphoreType.DMA((len(operands),)),
        ],
        compiler_params=params,
        cost_estimate=cost(10),
        name="near_rest",
    )(cluster_idx, branch_idx, pairs, *operands, near_part)


def solution(mesh):
    leaf3 = P(("branch", "cluster"), None, None)
    leaf2 = P(("branch", "cluster"), None)
    leaf4 = P(("branch", "cluster"), None, None, None)
    tree = P("branch", None, None, None, None)
    in_specs = (
        leaf3, leaf3, leaf2, leaf3, leaf3, leaf3, leaf3, leaf4,
        tree, tree, tree, P("branch", None, None, None), leaf2, leaf2,
    )
    return jax.shard_map(
        on_device, mesh=mesh, in_specs=in_specs, out_specs=leaf3, check_vma=False
    )
```

```python
import functools
import math

import jax
import jax.numpy as jnp
from jax import lax
from jax.experimental import pallas as pl
from jax.experimental.pallas import tpu as pltpu
from jax.sharding import PartitionSpec as P

f32, bf16 = jnp.float32, jnp.bfloat16
reg_square = 0.01
inv_four_pi = 0.25 / math.pi
dims = 3
ahead = 8
chunk = 2 * ahead
vmem = pl.BlockSpec(memory_space=pltpu.VMEM)
smem = pl.BlockSpec(memory_space=pltpu.SMEM)
anywhere = pl.BlockSpec(memory_space=pl.ANY)
params = pltpu.CompilerParams(vmem_limit_bytes=24 * 2**20)
large = pltpu.CompilerParams(vmem_limit_bytes=58 * 2**20)
lines = 4
depth = 6 * 2 * lines
fine, wide = jnp.float8_e4m3fn, jnp.float8_e5m2
entry_scale, fine_scale = 2.0**13, 2.0**15
own_steps = 5


def split(x):
    high = x.astype(bf16)
    return high, (x - high.astype(f32)).astype(bf16)


def split_three(x):
    high, rest = x.astype(bf16), None
    rest = x - high.astype(f32)
    middle = rest.astype(bf16)
    return high, middle, (rest - middle.astype(f32)).astype(bf16)


def dot_split(a, b, contract):
    rows = a.shape[0]
    a_high, a_low = split(a)
    b_high, b_low = split(b)
    numbers = (((1,), (contract,)), ((), ()))
    first = lax.dot_general(
        jnp.concatenate([a_high, a_low], axis=0), b_high, numbers, preferred_element_type=f32
    )
    second = lax.dot_general(a_high, b_low, numbers, preferred_element_type=f32)
    return first[:rows] + first[rows:] + second


def coord_tiles(pack_ref, first_row, tiles):
    return [pack_ref[first_row + 2 * lines * i : first_row + 2 * lines * (i + 1)] for i in range(tiles)]


def origin_tile(tiles):
    total = sum(jnp.sum(tile, axis=1, keepdims=True) for tile in tiles)
    total = total + pltpu.roll(total, lines, 0)
    return total * (1.0 / (2 * len(tiles) * tiles[0].shape[1]))


def centred(tile, origin):
    line = lax.broadcasted_iota(jnp.int32, tile.shape, 0) & (lines - 1)
    coords = (tile - origin) * (1.0 / entry_scale)
    square = coords * coords
    norm = pltpu.roll(square, 1, 0) + pltpu.roll(square, 2, 0) + pltpu.roll(square, 3, 0)
    return coords, norm, line == dims


def stage_sources(tiles, origin, source_ref, base):
    for i, tile in enumerate(tiles):
        coords, norm, spare = centred(tile, origin)
        high, middle, low = (x.astype(f32) for x in split_three(jnp.where(spare, norm, coords)))
        high_one, middle_one = jnp.where(spare, 1.0, high), jnp.where(spare, 1.0, middle)
        rows = jnp.concatenate([high, middle, high_one, low, high_one, middle_one], axis=0)
        source_ref[base + i] = rows.T.astype(bf16)


def stage_targets(tiles, origin, target_ref):
    for i, tile in enumerate(tiles):
        coords, norm, spare = centred(tile, origin)
        tile = jnp.where(spare, norm + reg_square / entry_scale**2, -2.0 * coords)
        high, middle, low = (x.astype(f32) for x in split_three(tile))
        high_one = jnp.where(spare, 1.0, high)
        rows = [
            high_one, high_one, jnp.where(spare, high, middle), high_one, jnp.where(spare, middle, low),
            jnp.where(spare, low, middle),
        ]
        first = lax.broadcasted_iota(jnp.int32, tile.shape, 0) < lines
        for half in range(2):
            mine = [jnp.where(first if half == 0 else jnp.logical_not(first), row, 0.0) for row in rows]
            other = [pltpu.roll(row, lines, 0) for row in mine]
            for place in range(2):
                chosen = mine if place == half else other
                target_ref[(2 * i + half) * 2 + place] = jnp.concatenate(chosen, axis=0).astype(bf16)


def stage_charge(weighted, charge_ref, tail_ref, slot):
    scen = weighted.shape[0]
    high, low = split(weighted * (1.0 / entry_scale))
    charge_ref[slot, :scen] = high
    charge_ref[slot, scen:] = low
    weighted = weighted * fine_scale
    high = weighted.astype(wide)
    low = (weighted - high.astype(f32)).astype(wide)
    tail_ref[slot] = jnp.concatenate([high.astype(f32), low.astype(f32)], axis=0).astype(wide)


def coef_place(leaf, scen, rank, panels, first_row):
    per_row = panels // rank
    row = first_row + leaf // per_row * scen
    lane = leaf % per_row * rank
    return slice(row, row + scen), slice(lane, lane + rank)


def prep_kernel(
    cluster_ref, branch_ref, charges_ref, coords_ref, areas_ref, col_ref, up_ref, transfer_ref, near_ref, far_ref,
    pack_ref, terms_ref, pairs_ref, target_ref, source_ref, charge_ref, tail_ref,
):
    leaves, scen, panels = charges_ref.shape
    rank = col_ref.shape[1]
    coord_row = leaves * scen
    coef_row = coord_row + leaves * lines

    path = None
    for level in range(transfer_ref.shape[1]):
        matrix = transfer_ref[0, level, (cluster_ref[0] >> level) & 1]
        path = matrix if path is None else dot_split(matrix, path, 0)

    for leaf in range(leaves):
        charge = charges_ref[leaf]
        weighted = charge * (areas_ref[leaf : leaf + 1] * inv_four_pi)
        pack_ref[leaf * scen : (leaf + 1) * scen] = weighted
        stage_charge(weighted, charge_ref, tail_ref, leaf)
        pack_ref[coef_place(leaf, scen, rank, panels, coef_row)] = dot_split(charge, col_ref[leaf], 1)
    node = jnp.zeros((scen, rank), f32)
    per_row = panels // rank
    for group in range(leaves // per_row):
        coefs = pack_ref[coef_row + group * scen : coef_row + (group + 1) * scen]
        ups = jnp.concatenate([up_ref[group * per_row + i] for i in range(per_row)], axis=1)
        node = node + dot_split(coefs, ups, 1)
    half = scen // 2
    node, root = (
        jnp.concatenate([x[:half], x[half:]], axis=1) for x in (node, dot_split(node, path, 1))
    )
    branches = terms_ref.shape[0]
    for branch in range(branches):
        term = jnp.where(branch == branch_ref[0], node, root)
        for cluster in range(terms_ref.shape[1]):
            terms_ref[branch, cluster] = term
    nothing = jnp.zeros((1, panels), f32)
    for leaf in range(leaves):
        rows = [coords_ref[axis, leaf : leaf + 1] for axis in range(dims)] + [nothing]
        pack_ref[coord_row + lines * leaf : coord_row + lines * (leaf + 1)] = jnp.concatenate(rows, axis=0)
    tiles = coord_tiles(pack_ref, coord_row, leaves // 2)
    origin = origin_tile(tiles)
    stage_targets(tiles, origin, target_ref)
    stage_sources(tiles, origin, source_ref, 0)

    slots = near_ref.shape[1]
    count = leaves * slots
    near = near_ref[...]
    base = near[0:1, 0:1] - leaves

    def flat(table):
        n = table.shape[1]
        spread = jnp.where(
            lax.rem(lax.broadcasted_iota(jnp.int32, (n, count), 1), n)
            == lax.broadcasted_iota(jnp.int32, (n, count), 0), 1.0, 0.0
        )
        wide = jnp.dot(table.astype(f32).astype(bf16), spread.astype(bf16), preferred_element_type=f32)
        mine = lax.broadcasted_iota(jnp.int32, (leaves, count), 1) // n == lax.broadcasted_iota(
            jnp.int32, (leaves, count), 0
        )
        return jnp.sum(jnp.where(mine, wide, 0.0), axis=0, keepdims=True)

    source = flat(near - base)
    partners = far_ref.shape[0]
    far_slots = far_ref[...].astype(jnp.int32) - jnp.broadcast_to(base, far_ref.shape)
    own_rows = jnp.broadcast_to(
        jnp.where((source >= leaves) & (source < 2 * leaves), 1.0, 0.0), (8, count)
    )
    rows = lax.broadcasted_iota(jnp.int32, (count, count), 0)
    cols = lax.broadcasted_iota(jnp.int32, (count, count), 1)
    earlier = jnp.where(rows < cols, 1.0, 0.0).astype(bf16)
    own_before = jnp.dot(own_rows.astype(bf16), earlier, preferred_element_type=f32)
    total = jnp.sum(own_rows, axis=1, keepdims=True)
    index = lax.broadcasted_iota(jnp.int32, (8, count), 1)
    spot = jnp.where(own_rows > 0.0, own_before, total + index.astype(f32) - own_before)
    chosen = jnp.where(rows == spot[:1].astype(jnp.int32), 1.0, 0.0).astype(bf16)
    kind = lax.broadcasted_iota(jnp.int32, (8, count), 0)
    values = jnp.where(kind == 0, (index // slots).astype(f32), jnp.broadcast_to(source, (8, count)))
    values = lax.dot_general(
        values.astype(bf16), chosen, (((1,), (1,)), ((), ())), preferred_element_type=f32
    )
    pairs_ref[...] = jnp.where(kind == 2, total, values).astype(jnp.int32)
    pairs_ref[4 : 4 + partners, :leaves] = far_slots


def near_pairs(some, begin, end, base_slot, pairs_ref, target_ref, source_ref, charge_ref, tail_ref, out_ref, high_ref, low_ref):
    scen = out_ref.shape[1]

    def generate(pair, slot):
        source = pairs_ref[1, pair] - base_slot
        square = jnp.dot(
            source_ref[source >> 1],
            target_ref[2 * pairs_ref[0, pair] + (source & 1)],
            preferred_element_type=f32,
        )
        entry = lax.rsqrt(square)
        high = entry.astype(bf16)
        high_ref[slot] = high
        low_ref[slot] = (entry - high.astype(f32)).astype(fine)

    def apply(pair, slot):
        target = pairs_ref[0, pair]
        source = pairs_ref[1, pair] - base_slot
        first = jnp.dot(charge_ref[source], high_ref[slot], preferred_element_type=f32)
        second = jnp.dot(tail_ref[source], low_ref[slot], preferred_element_type=f32)
        out_ref[target] += (
            first[:scen] + first[scen:] + (second[:scen] + second[scen:]) * (1.0 / (entry_scale * fine_scale))
        )

    def run():
        for step in range(ahead):
            generate(begin * chunk + step, step)

        def body(step, carry):
            for half in range(2):
                base = step * chunk + half * ahead
                for lane in range(ahead):
                    generate(base + ahead + lane, (1 - half) * ahead + lane)
                    apply(base + lane, half * ahead + lane)
            return carry

        lax.fori_loop(begin, end - 1, body, 0)
        base = (end - 1) * chunk
        for lane in range(ahead):
            generate(base + ahead + lane, ahead + lane)
            apply(base + lane, lane)
        for lane in range(ahead):
            apply(base + ahead + lane, ahead + lane)

    if some:
        run()
    else:
        pl.when(begin < end)(run)


def own_chunks(pairs_ref):
    return jnp.minimum(own_steps, pairs_ref[2, 0] // chunk)


def own_kernel(pairs_ref, target_ref, source_ref, charge_ref, tail_ref, out_ref, high_ref, low_ref):
    out_ref[...] = jnp.zeros_like(out_ref)
    near_pairs(
        out_ref.shape[0] >= chunk, 0, own_chunks(pairs_ref), out_ref.shape[0], pairs_ref, target_ref, source_ref, charge_ref,
        tail_ref, out_ref, high_ref, low_ref,
    )


def rest_kernel(
    cluster_ref, branch_idx_ref, pairs_ref, own_any, chip_any, side_any, coupling_any, terms_any,
    up_any, down_any, sibling_any, branch_any, leaf_down_any, row_any, start_ref, out_ref,
    own_ref, chip_ref, side_ref, coupling_ref, terms_ref, up_ref, down_ref, sibling_ref, branch_ref,
    leaf_down_ref, row_ref, target_ref, source_ref, charge_ref, tail_ref, coef_ref, high_ref, low_ref, sems,
):
    leaves, scen, panels = out_ref.shape
    rank = leaf_down_ref.shape[1]
    branches, clusters = terms_ref.shape[:2]
    levels = up_ref.shape[1]
    coord_row = leaves * scen
    coef_row = coord_row + leaves * lines
    cluster_idx, branch_idx = cluster_ref[0], branch_idx_ref[0]
    refs = (
        own_any, chip_any, side_any, terms_any, up_any, down_any, sibling_any, branch_any, coupling_any,
        leaf_down_any, row_any,
    )
    held = (
        own_ref, chip_ref, side_ref, terms_ref, up_ref, down_ref, sibling_ref, branch_ref, coupling_ref,
        leaf_down_ref, row_ref,
    )
    copies = [pltpu.make_async_copy(ref, to, sems.at[i]) for i, (ref, to) in enumerate(zip(refs, held))]
    for copy in copies:
        copy.start()
    copies[0].wait()
    tiles = coord_tiles(own_ref, coord_row, leaves // 2)
    origin = origin_tile(tiles)
    stage_targets(tiles, origin, target_ref)
    odd = cluster_idx & 1
    for i, (pack_ref, place) in enumerate(((own_ref, 1), (chip_ref, 2 - 2 * odd), (side_ref, 2 * odd))):
        if i:
            copies[i].wait()
        stage_sources(coord_tiles(pack_ref, coord_row, leaves // 2), origin, source_ref, place * (leaves // 2))
        base = place * leaves
        for leaf in range(leaves):
            stage_charge(pack_ref[leaf * scen : (leaf + 1) * scen], charge_ref, tail_ref, base + leaf)
            coef_ref[base + leaf] = pack_ref[coef_place(leaf, scen, rank, panels, coef_row)]
    out_ref[...] = start_ref[...]
    near_pairs(
        False, own_chunks(pairs_ref), pairs_ref.shape[1] // chunk, 0, pairs_ref, target_ref, source_ref,
        charge_ref, tail_ref, out_ref, high_ref, low_ref,
    )
    for copy in copies[3:]:
        copy.wait()

    def unfold(x):
        return jnp.concatenate([x[..., :rank], x[..., rank:]], axis=-2)

    current = unfold(terms_ref[branch_idx])
    sums, chains, chain = [], [], None
    for level in range(levels):
        width = clusters >> level
        chosen = lax.broadcasted_iota(jnp.int32, (width, 1, 1), 0) == (cluster_idx >> level) ^ 1
        sums.append(jnp.sum(jnp.where(chosen, current, 0.0), axis=0))
        if level + 1 < levels:
            couples = current.reshape(width // 2, 2 * scen, rank)
            sides = [
                couples[:, side * scen : (side + 1) * scen].reshape(width // 2 * scen, rank)
                for side in range(2)
            ]
            current = dot_split(sides[0], up_ref[0, level, 0], 1) + dot_split(
                sides[1], up_ref[0, level, 1], 1
            )
            current = current.reshape(width // 2, scen, rank)
        parity = (cluster_idx >> level) & 1
        matrix = sibling_ref[0, level, parity]
        chains.append(matrix if chain is None else dot_split(chain, matrix, 0))
        matrix = down_ref[0, level, parity]
        chain = matrix if chain is None else dot_split(chain, matrix, 0)
    for other in range(branches - 1):
        partner = lax.rem(branch_idx + 1 + other, branches)
        sums.append(unfold(jnp.sum(terms_ref[partner], axis=0)))
        chains.append(dot_split(chain, branch_ref[0, other], 0))
    downward = jnp.zeros((scen, rank), f32)
    for term, matrix in zip(sums, chains):
        downward = downward + dot_split(term, matrix, 1)

    for leaf in range(leaves):
        partners = range(coupling_ref.shape[1])
        coefs = jnp.concatenate([coef_ref[pairs_ref[4 + partner, leaf]] for partner in partners], axis=1)
        matrices = jnp.concatenate([coupling_ref[leaf, partner] for partner in partners], axis=1)
        total = dot_split(coefs, matrices, 1) + dot_split(downward, leaf_down_ref[leaf], 1)
        out_ref[leaf] += dot_split(total, row_ref[leaf], 0)


def on_device(
    charges, coords, areas, col_basis, row_basis, leaf_up, leaf_down, leaf_coupling,
    up_transfer, down_transfer, sibling_coupling, branch_coupling, near_list, far_list,
):
    leaves, scen, panels = charges.shape
    rank = col_basis.shape[1]
    clusters, branches = lax.axis_size("cluster"), lax.axis_size("branch")
    cluster_idx = lax.axis_index("cluster").reshape(1).astype(jnp.int32)
    branch_idx = lax.axis_index("branch").reshape(1).astype(jnp.int32)
    count = near_list.size
    pack_rows = leaves * scen + leaves * lines + leaves * scen * rank // panels

    def stages(places):
        return (
            pltpu.VMEM((places * leaves // 2, panels, depth), bf16),
            pltpu.VMEM((places * leaves, 2 * scen, panels), bf16),
            pltpu.VMEM((places * leaves, 2 * scen, panels), wide),
        )

    slots = [pltpu.VMEM((chunk, panels, panels), kind) for kind in (bf16, fine)]
    terms_shape = (branches, clusters, scen // 2, 2 * rank)
    pack, terms, pairs, target, *own_stages = pl.pallas_call(
        prep_kernel,
        out_shape=(
            jax.ShapeDtypeStruct((pack_rows, panels), f32),
            jax.ShapeDtypeStruct(terms_shape, f32),
            jax.ShapeDtypeStruct((8, count), jnp.int32),
            pltpu.VMEM((2 * leaves, depth, panels), bf16),
            *stages(1),
        ),
        in_specs=[smem] * 2 + [vmem] * 8,
        out_specs=(vmem,) * 7,
        compiler_params=large,
        name="prep",
    )(
        cluster_idx, branch_idx, charges, coords.transpose(1, 0, 2), areas, col_basis, leaf_up, up_transfer,
        near_list, far_list.T,
    )

    chip = lax.ppermute(pack, "cluster", [(i, i ^ 1) for i in range(clusters)])
    across = [(i, i + 1) for i in range(1, clusters - 1, 2)]
    side = lax.ppermute(pack, "cluster", across + [(j, i) for i, j in across])
    terms = terms.reshape(branches * clusters, scen // 2, 2 * rank)
    terms = lax.all_to_all(terms, ("branch", "cluster"), 0, 0, tiled=True)
    terms = terms.reshape(terms_shape)

    kept = pltpu.VMEM((leaves, scen, panels), f32)
    entries = count * panels * panels

    def cost(share):
        return pl.CostEstimate(
            flops=int(entries * 80 * share), bytes_accessed=2**20, transcendentals=int(entries * share)
        )

    stay = functools.partial(pltpu.with_memory_space_constraint, memory_space=pltpu.HBM)
    pairs = stay(pairs)
    near_part = pl.pallas_call(
        own_kernel,
        out_shape=kept,
        in_specs=[smem] + [vmem] * 4,
        out_specs=vmem,
        scratch_shapes=slots,
        compiler_params=params,
        cost_estimate=cost(10),
        name="near_own",
    )(pairs, target, *own_stages)
    operands = (
        stay(pack), chip, side, stay(leaf_coupling), terms, stay(up_transfer), stay(down_transfer),
        stay(sibling_coupling), stay(branch_coupling), stay(leaf_down), stay(row_basis),
    )
    return pl.pallas_call(
        rest_kernel,
        out_shape=jax.ShapeDtypeStruct((leaves, scen, panels), f32),
        in_specs=[smem] * 3 + [anywhere] * len(operands) + [vmem],
        out_specs=vmem,
        scratch_shapes=[
            *(pltpu.VMEM(operand.shape, f32) for operand in operands),
            pltpu.VMEM((2 * leaves, depth, panels), bf16),
            *stages(3),
            pltpu.VMEM((3 * leaves, scen, rank), f32),
            *slots,
            pltpu.SemaphoreType.DMA((len(operands),)),
        ],
        compiler_params=params,
        cost_estimate=cost(10),
        name="near_rest",
    )(cluster_idx, branch_idx, pairs, *operands, near_part)


def solution(mesh):
    leaf3 = P(("branch", "cluster"), None, None)
    leaf2 = P(("branch", "cluster"), None)
    leaf4 = P(("branch", "cluster"), None, None, None)
    tree = P("branch", None, None, None, None)
    in_specs = (
        leaf3, leaf3, leaf2, leaf3, leaf3, leaf3, leaf3, leaf4,
        tree, tree, tree, P("branch", None, None, None), leaf2, leaf2,
    )
    return jax.shard_map(
        on_device, mesh=mesh, in_specs=in_specs, out_specs=leaf3, check_vma=False
    )
```

```python
import functools
import math

import jax
import jax.numpy as jnp
from jax import lax
from jax.experimental import pallas as pl
from jax.experimental.pallas import tpu as pltpu
from jax.sharding import PartitionSpec as P

f32, bf16 = jnp.float32, jnp.bfloat16
reg_square = 0.01
inv_four_pi = 0.25 / math.pi
dims = 3
ahead = 8
chunk = 2 * ahead
vmem = pl.BlockSpec(memory_space=pltpu.VMEM)
smem = pl.BlockSpec(memory_space=pltpu.SMEM)
anywhere = pl.BlockSpec(memory_space=pl.ANY)
params = pltpu.CompilerParams(vmem_limit_bytes=24 * 2**20)
large = pltpu.CompilerParams(vmem_limit_bytes=58 * 2**20)
lines = 4
depth = 6 * 2 * lines
fine, wide = jnp.float8_e4m3fn, jnp.float8_e5m2
entry_scale, fine_scale = 2.0**13, 2.0**15
chip_steps = 8


def split(x):
    high = x.astype(bf16)
    return high, (x - high.astype(f32)).astype(bf16)


def split_three(x):
    high, rest = x.astype(bf16), None
    rest = x - high.astype(f32)
    middle = rest.astype(bf16)
    return high, middle, (rest - middle.astype(f32)).astype(bf16)


def dot_split(a, b, contract):
    rows = a.shape[0]
    a_high, a_low = split(a)
    b_high, b_low = split(b)
    numbers = (((1,), (contract,)), ((), ()))
    first = lax.dot_general(
        jnp.concatenate([a_high, a_low], axis=0), b_high, numbers, preferred_element_type=f32
    )
    second = lax.dot_general(a_high, b_low, numbers, preferred_element_type=f32)
    return first[:rows] + first[rows:] + second


def coord_tiles(pack_ref, first_row, tiles):
    return [pack_ref[first_row + 2 * lines * i : first_row + 2 * lines * (i + 1)] for i in range(tiles)]


def origin_tile(tiles):
    total = sum(jnp.sum(tile, axis=1, keepdims=True) for tile in tiles)
    total = total + pltpu.roll(total, lines, 0)
    return total * (1.0 / (2 * len(tiles) * tiles[0].shape[1]))


def centred(tile, origin):
    line = lax.broadcasted_iota(jnp.int32, tile.shape, 0) & (lines - 1)
    coords = (tile - origin) * (1.0 / entry_scale)
    square = coords * coords
    norm = pltpu.roll(square, 1, 0) + pltpu.roll(square, 2, 0) + pltpu.roll(square, 3, 0)
    return coords, norm, line == dims


def stage_sources(tiles, origin, source_ref, base):
    for i, tile in enumerate(tiles):
        coords, norm, spare = centred(tile, origin)
        high, middle, low = (x.astype(f32) for x in split_three(jnp.where(spare, norm, coords)))
        high_one, middle_one = jnp.where(spare, 1.0, high), jnp.where(spare, 1.0, middle)
        rows = jnp.concatenate([high, middle, high_one, low, high_one, middle_one], axis=0)
        source_ref[base + i] = rows.T.astype(bf16)


def stage_targets(tiles, origin, target_ref):
    for i, tile in enumerate(tiles):
        coords, norm, spare = centred(tile, origin)
        tile = jnp.where(spare, norm + reg_square / entry_scale**2, -2.0 * coords)
        high, middle, low = (x.astype(f32) for x in split_three(tile))
        high_one = jnp.where(spare, 1.0, high)
        rows = [
            high_one, high_one, jnp.where(spare, high, middle), high_one, jnp.where(spare, middle, low),
            jnp.where(spare, low, middle),
        ]
        first = lax.broadcasted_iota(jnp.int32, tile.shape, 0) < lines
        for half in range(2):
            mine = [jnp.where(first if half == 0 else jnp.logical_not(first), row, 0.0) for row in rows]
            other = [pltpu.roll(row, lines, 0) for row in mine]
            for place in range(2):
                chosen = mine if place == half else other
                target_ref[(2 * i + half) * 2 + place] = jnp.concatenate(chosen, axis=0).astype(bf16)


def stage_charge(weighted, charge_ref, tail_ref, slot):
    scen = weighted.shape[0]
    high, low = split(weighted * (1.0 / entry_scale))
    charge_ref[slot, :scen] = high
    charge_ref[slot, scen:] = low
    weighted = weighted * fine_scale
    high = weighted.astype(wide)
    low = (weighted - high.astype(f32)).astype(wide)
    tail_ref[slot] = jnp.concatenate([high.astype(f32), low.astype(f32)], axis=0).astype(wide)


def coef_place(leaf, scen, rank, panels, first_row):
    per_row = panels // rank
    row = first_row + leaf // per_row * scen
    lane = leaf % per_row * rank
    return slice(row, row + scen), slice(lane, lane + rank)


def prep_kernel(
    cluster_ref, branch_ref, charges_ref, coords_ref, areas_ref, col_ref, up_ref, transfer_ref, near_ref, far_ref,
    pack_ref, terms_ref, pairs_ref,
):
    leaves, scen, panels = charges_ref.shape
    rank = col_ref.shape[1]
    coord_row = leaves * scen
    coef_row = coord_row + leaves * lines

    path = None
    for level in range(transfer_ref.shape[1]):
        matrix = transfer_ref[0, level, (cluster_ref[0] >> level) & 1]
        path = matrix if path is None else dot_split(matrix, path, 0)

    for leaf in range(leaves):
        charge = charges_ref[leaf]
        weighted = charge * (areas_ref[leaf : leaf + 1] * inv_four_pi)
        pack_ref[leaf * scen : (leaf + 1) * scen] = weighted
        pack_ref[coef_place(leaf, scen, rank, panels, coef_row)] = dot_split(charge, col_ref[leaf], 1)
    node = jnp.zeros((scen, rank), f32)
    per_row = panels // rank
    for group in range(leaves // per_row):
        coefs = pack_ref[coef_row + group * scen : coef_row + (group + 1) * scen]
        ups = jnp.concatenate([up_ref[group * per_row + i] for i in range(per_row)], axis=1)
        node = node + dot_split(coefs, ups, 1)
    half = scen // 2
    node, root = (
        jnp.concatenate([x[:half], x[half:]], axis=1) for x in (node, dot_split(node, path, 1))
    )
    branches = terms_ref.shape[0]
    for branch in range(branches):
        term = jnp.where(branch == branch_ref[0], node, root)
        for cluster in range(terms_ref.shape[1]):
            terms_ref[branch, cluster] = term
    nothing = jnp.zeros((1, panels), f32)
    for leaf in range(leaves):
        rows = [coords_ref[axis, leaf : leaf + 1] for axis in range(dims)] + [nothing]
        pack_ref[coord_row + lines * leaf : coord_row + lines * (leaf + 1)] = jnp.concatenate(rows, axis=0)
    slots = near_ref.shape[1]
    count = leaves * slots
    near = near_ref[...]
    base = near[0:1, 0:1] - leaves

    def flat(table):
        n = table.shape[1]
        spread = jnp.where(
            lax.rem(lax.broadcasted_iota(jnp.int32, (n, count), 1), n)
            == lax.broadcasted_iota(jnp.int32, (n, count), 0), 1.0, 0.0
        )
        wide = jnp.dot(table.astype(f32).astype(bf16), spread.astype(bf16), preferred_element_type=f32)
        mine = lax.broadcasted_iota(jnp.int32, (leaves, count), 1) // n == lax.broadcasted_iota(
            jnp.int32, (leaves, count), 0
        )
        return jnp.sum(jnp.where(mine, wide, 0.0), axis=0, keepdims=True)

    source = flat(near - base)
    partners = far_ref.shape[0]
    far_slots = far_ref[...].astype(jnp.int32) - jnp.broadcast_to(base, far_ref.shape)
    first = (leaves * (1 - (cluster_ref[0] & 1))).astype(f32)
    chip_rows = jnp.broadcast_to(
        jnp.where((source >= first) & (source < first + 2 * leaves), 1.0, 0.0), (8, count)
    )
    rows = lax.broadcasted_iota(jnp.int32, (count, count), 0)
    cols = lax.broadcasted_iota(jnp.int32, (count, count), 1)
    earlier = jnp.where(rows < cols, 1.0, 0.0).astype(bf16)
    chip_before = jnp.dot(chip_rows.astype(bf16), earlier, preferred_element_type=f32)
    total = jnp.sum(chip_rows, axis=1, keepdims=True)
    index = lax.broadcasted_iota(jnp.int32, (8, count), 1)
    spot = jnp.where(chip_rows > 0.0, chip_before, total + index.astype(f32) - chip_before)
    chosen = jnp.where(rows == spot[:1].astype(jnp.int32), 1.0, 0.0).astype(bf16)
    kind = lax.broadcasted_iota(jnp.int32, (8, count), 0)
    values = jnp.where(kind == 0, (index // slots).astype(f32), jnp.broadcast_to(source, (8, count)))
    values = lax.dot_general(
        values.astype(bf16), chosen, (((1,), (1,)), ((), ())), preferred_element_type=f32
    )
    pairs_ref[...] = jnp.where(kind == 2, total, values).astype(jnp.int32)
    pairs_ref[4 : 4 + partners, :leaves] = far_slots


def near_pairs(some, begin, end, base_slot, pairs_ref, target_ref, source_ref, charge_ref, tail_ref, out_ref, high_ref, low_ref):
    scen = out_ref.shape[1]

    def generate(pair, slot):
        source = pairs_ref[1, pair] - base_slot
        square = jnp.dot(
            source_ref[source >> 1],
            target_ref[2 * pairs_ref[0, pair] + (source & 1)],
            preferred_element_type=f32,
        )
        entry = lax.rsqrt(square)
        high = entry.astype(bf16)
        high_ref[slot] = high
        low_ref[slot] = (entry - high.astype(f32)).astype(fine)

    def apply(pair, slot):
        target = pairs_ref[0, pair]
        source = pairs_ref[1, pair] - base_slot
        first = jnp.dot(charge_ref[source], high_ref[slot], preferred_element_type=f32)
        second = jnp.dot(tail_ref[source], low_ref[slot], preferred_element_type=f32)
        out_ref[target] += (
            first[:scen] + first[scen:] + (second[:scen] + second[scen:]) * (1.0 / (entry_scale * fine_scale))
        )

    def run():
        for step in range(ahead):
            generate(begin * chunk + step, step)

        def body(step, carry):
            for half in range(2):
                base = step * chunk + half * ahead
                for lane in range(ahead):
                    generate(base + ahead + lane, (1 - half) * ahead + lane)
                    apply(base + lane, half * ahead + lane)
            return carry

        lax.fori_loop(begin, end - 1, body, 0)
        base = (end - 1) * chunk
        for lane in range(ahead):
            generate(base + ahead + lane, ahead + lane)
            apply(base + lane, lane)
        for lane in range(ahead):
            apply(base + ahead + lane, ahead + lane)

    if some:
        run()
    else:
        pl.when(begin < end)(run)


def chip_chunks(pairs_ref):
    return jnp.minimum(chip_steps, pairs_ref[2, 0] // chunk)


def chip_kernel(
    cluster_ref, pairs_ref, own_any, chip_any, out_ref, own_ref, chip_ref, target_ref, source_ref, charge_ref,
    tail_ref, high_ref, low_ref, sems,
):
    leaves, scen, panels = out_ref.shape
    coord_row = leaves * scen
    copies = [
        pltpu.make_async_copy(ref, to, sems.at[i])
        for i, (ref, to) in enumerate(((own_any, own_ref), (chip_any, chip_ref)))
    ]
    for copy in copies:
        copy.start()
    out_ref[...] = jnp.zeros_like(out_ref)
    copies[0].wait()
    tiles = coord_tiles(own_ref, coord_row, leaves // 2)
    origin = origin_tile(tiles)
    stage_targets(tiles, origin, target_ref)
    odd = cluster_ref[0] & 1
    for i, (pack_ref, place) in enumerate(((own_ref, 1), (chip_ref, 2 - 2 * odd))):
        if i:
            copies[i].wait()
        stage_sources(coord_tiles(pack_ref, coord_row, leaves // 2), origin, source_ref, place * (leaves // 2))
        base = place * leaves
        for leaf in range(leaves):
            stage_charge(pack_ref[leaf * scen : (leaf + 1) * scen], charge_ref, tail_ref, base + leaf)
    near_pairs(
        leaves >= chunk, 0, chip_chunks(pairs_ref), 0, pairs_ref, target_ref, source_ref, charge_ref,
        tail_ref, out_ref, high_ref, low_ref,
    )


def rest_kernel(
    cluster_ref, branch_idx_ref, pairs_ref, own_any, chip_any, side_any, coupling_any, terms_any,
    up_any, down_any, sibling_any, branch_any, leaf_down_any, row_any, start_ref, out_ref,
    own_ref, chip_ref, side_ref, coupling_ref, terms_ref, up_ref, down_ref, sibling_ref, branch_ref,
    leaf_down_ref, row_ref, target_ref, source_ref, charge_ref, tail_ref, coef_ref, high_ref, low_ref, sems,
):
    leaves, scen, panels = out_ref.shape
    rank = leaf_down_ref.shape[1]
    branches, clusters = terms_ref.shape[:2]
    levels = up_ref.shape[1]
    coord_row = leaves * scen
    coef_row = coord_row + leaves * lines
    cluster_idx, branch_idx = cluster_ref[0], branch_idx_ref[0]
    refs = (
        own_any, chip_any, side_any, terms_any, up_any, down_any, sibling_any, branch_any, coupling_any,
        leaf_down_any, row_any,
    )
    held = (
        own_ref, chip_ref, side_ref, terms_ref, up_ref, down_ref, sibling_ref, branch_ref, coupling_ref,
        leaf_down_ref, row_ref,
    )
    copies = [pltpu.make_async_copy(ref, to, sems.at[i]) for i, (ref, to) in enumerate(zip(refs, held))]
    for copy in copies:
        copy.start()
    copies[0].wait()
    tiles = coord_tiles(own_ref, coord_row, leaves // 2)
    origin = origin_tile(tiles)
    stage_targets(tiles, origin, target_ref)
    odd = cluster_idx & 1
    for i, (pack_ref, place) in enumerate(((own_ref, 1), (chip_ref, 2 - 2 * odd), (side_ref, 2 * odd))):
        if i:
            copies[i].wait()
        stage_sources(coord_tiles(pack_ref, coord_row, leaves // 2), origin, source_ref, place * (leaves // 2))
        base = place * leaves
        for leaf in range(leaves):
            stage_charge(pack_ref[leaf * scen : (leaf + 1) * scen], charge_ref, tail_ref, base + leaf)
            coef_ref[base + leaf] = pack_ref[coef_place(leaf, scen, rank, panels, coef_row)]
    out_ref[...] = start_ref[...]
    near_pairs(
        False, chip_chunks(pairs_ref), pairs_ref.shape[1] // chunk, 0, pairs_ref, target_ref, source_ref,
        charge_ref, tail_ref, out_ref, high_ref, low_ref,
    )
    for copy in copies[3:]:
        copy.wait()

    def unfold(x):
        return jnp.concatenate([x[..., :rank], x[..., rank:]], axis=-2)

    current = unfold(terms_ref[branch_idx])
    sums, chains, chain = [], [], None
    for level in range(levels):
        width = clusters >> level
        chosen = lax.broadcasted_iota(jnp.int32, (width, 1, 1), 0) == (cluster_idx >> level) ^ 1
        sums.append(jnp.sum(jnp.where(chosen, current, 0.0), axis=0))
        if level + 1 < levels:
            couples = current.reshape(width // 2, 2 * scen, rank)
            sides = [
                couples[:, side * scen : (side + 1) * scen].reshape(width // 2 * scen, rank)
                for side in range(2)
            ]
            current = dot_split(sides[0], up_ref[0, level, 0], 1) + dot_split(
                sides[1], up_ref[0, level, 1], 1
            )
            current = current.reshape(width // 2, scen, rank)
        parity = (cluster_idx >> level) & 1
        matrix = sibling_ref[0, level, parity]
        chains.append(matrix if chain is None else dot_split(chain, matrix, 0))
        matrix = down_ref[0, level, parity]
        chain = matrix if chain is None else dot_split(chain, matrix, 0)
    for other in range(branches - 1):
        partner = lax.rem(branch_idx + 1 + other, branches)
        sums.append(unfold(jnp.sum(terms_ref[partner], axis=0)))
        chains.append(dot_split(chain, branch_ref[0, other], 0))
    downward = jnp.zeros((scen, rank), f32)
    for term, matrix in zip(sums, chains):
        downward = downward + dot_split(term, matrix, 1)

    for leaf in range(leaves):
        partners = range(coupling_ref.shape[1])
        coefs = jnp.concatenate([coef_ref[pairs_ref[4 + partner, leaf]] for partner in partners], axis=1)
        matrices = jnp.concatenate([coupling_ref[leaf, partner] for partner in partners], axis=1)
        total = dot_split(coefs, matrices, 1) + dot_split(downward, leaf_down_ref[leaf], 1)
        out_ref[leaf] += dot_split(total, row_ref[leaf], 0)


def on_device(
    charges, coords, areas, col_basis, row_basis, leaf_up, leaf_down, leaf_coupling,
    up_transfer, down_transfer, sibling_coupling, branch_coupling, near_list, far_list,
):
    leaves, scen, panels = charges.shape
    rank = col_basis.shape[1]
    clusters, branches = lax.axis_size("cluster"), lax.axis_size("branch")
    cluster_idx = lax.axis_index("cluster").reshape(1).astype(jnp.int32)
    branch_idx = lax.axis_index("branch").reshape(1).astype(jnp.int32)
    count = near_list.size
    pack_rows = leaves * scen + leaves * lines + leaves * scen * rank // panels

    staged = [
        pltpu.VMEM((2 * leaves, depth, panels), bf16),
        pltpu.VMEM((3 * leaves // 2, panels, depth), bf16),
        pltpu.VMEM((3 * leaves, 2 * scen, panels), bf16),
        pltpu.VMEM((3 * leaves, 2 * scen, panels), wide),
    ]
    slots = [pltpu.VMEM((chunk, panels, panels), kind) for kind in (bf16, fine)]
    terms_shape = (branches, clusters, scen // 2, 2 * rank)
    pack, terms, pairs = pl.pallas_call(
        prep_kernel,
        out_shape=(
            jax.ShapeDtypeStruct((pack_rows, panels), f32),
            jax.ShapeDtypeStruct(terms_shape, f32),
            jax.ShapeDtypeStruct((8, count), jnp.int32),
        ),
        in_specs=[smem] * 2 + [vmem] * 8,
        out_specs=(vmem,) * 3,
        compiler_params=large,
        name="prep",
    )(
        cluster_idx, branch_idx, charges, coords.transpose(1, 0, 2), areas, col_basis, leaf_up, up_transfer,
        near_list, far_list.T,
    )

    chip = lax.ppermute(pack, "cluster", [(i, i ^ 1) for i in range(clusters)])
    across = [(i, i + 1) for i in range(1, clusters - 1, 2)]
    side = lax.ppermute(pack, "cluster", across + [(j, i) for i, j in across])
    terms = terms.reshape(branches * clusters, scen // 2, 2 * rank)
    terms = lax.all_to_all(terms, ("branch", "cluster"), 0, 0, tiled=True)
    terms = terms.reshape(terms_shape)

    kept = pltpu.VMEM((leaves, scen, panels), f32)
    entries = count * panels * panels

    def cost(share):
        return pl.CostEstimate(
            flops=int(entries * 80 * share), bytes_accessed=2**20, transcendentals=int(entries * share)
        )

    stay = functools.partial(pltpu.with_memory_space_constraint, memory_space=pltpu.HBM)
    pairs = stay(pairs)
    near_part = pl.pallas_call(
        chip_kernel,
        out_shape=kept,
        in_specs=[smem] * 2 + [anywhere] * 2,
        out_specs=vmem,
        scratch_shapes=[
            pltpu.VMEM(pack.shape, f32),
            pltpu.VMEM(pack.shape, f32),
            *staged,
            *slots,
            pltpu.SemaphoreType.DMA((2,)),
        ],
        compiler_params=params,
        cost_estimate=cost(10),
        name="near_chip",
    )(cluster_idx, pairs, stay(pack), chip)
    operands = (
        stay(pack), chip, side, stay(leaf_coupling), terms, stay(up_transfer), stay(down_transfer),
        stay(sibling_coupling), stay(branch_coupling), stay(leaf_down), stay(row_basis),
    )
    return pl.pallas_call(
        rest_kernel,
        out_shape=jax.ShapeDtypeStruct((leaves, scen, panels), f32),
        in_specs=[smem] * 3 + [anywhere] * len(operands) + [vmem],
        out_specs=vmem,
        scratch_shapes=[
            *(pltpu.VMEM(operand.shape, f32) for operand in operands),
            *staged,
            pltpu.VMEM((3 * leaves, scen, rank), f32),
            *slots,
            pltpu.SemaphoreType.DMA((len(operands),)),
        ],
        compiler_params=params,
        cost_estimate=cost(10),
        name="near_rest",
    )(cluster_idx, branch_idx, pairs, *operands, near_part)


def solution(mesh):
    leaf3 = P(("branch", "cluster"), None, None)
    leaf2 = P(("branch", "cluster"), None)
    leaf4 = P(("branch", "cluster"), None, None, None)
    tree = P("branch", None, None, None, None)
    in_specs = (
        leaf3, leaf3, leaf2, leaf3, leaf3, leaf3, leaf3, leaf4,
        tree, tree, tree, P("branch", None, None, None), leaf2, leaf2,
    )
    return jax.shard_map(
        on_device, mesh=mesh, in_specs=in_specs, out_specs=leaf3, check_vma=False
    )
```
